32 devices in a mesh: groups: 2 (over y), hx: 16 (over z, x, core).
Axes of the slice: x: 2, y: 2, z: 4, core: 2. Of those that a mesh axis runs over, the one named last changes fastest.
Arguments:
- tokens: bfloat16 [32, 8192], P(('groups', 'hx')), parts along dimension 0, may hold values from -6 to 6
- gate_codes: bfloat16 [8192, 26624], P(None, 'hx'), may hold values from -8 to 7, as said below
- gate_scales: float32 [64, 26624], P(None, 'hx'), may hold values from 0.00077339803 to 0.00773398
- up_codes: bfloat16 [8192, 26624], P(None, 'hx'), may hold values from -8 to 7, as said below
- up_scales: float32 [64, 26624], P(None, 'hx'), may hold values from 0.00077339803 to 0.00773398
- down_codes: bfloat16 [26624, 8192], P('hx'), may hold values from -8 to 7, as said below
- down_scales: float32 [8192], replicated, may hold values from 0.00061286293 to 0.006128629
- hadamard: int32 [52, 52], replicated, may hold values from -1 to 1, as said below
Outputs:
- mixed: bfloat16 [32, 8192], P(('groups', 'hx')), parts along dimension 0
The draws below stay inside these ranges and needn't reach their ends.
There are 2 independent parts, one for each index of `groups`. The reference program is written for one: setup_inputs(seed, part) draws one part's arguments, and reference() takes and returns one part's arrays. A program takes and returns all parts, laid end to end along the dimension named above; an argument that names none is the same for every part. Nothing has to cross between parts.
Inputs may be any that keep to these rules, and one draw needn't show every extreme that they name: `gate_codes`: whole numbers. `up_codes`: whole numbers. `down_codes`: whole numbers. `hadamard`: a Hadamard matrix: every entry is -1 or 1 and any two rows are orthogonal.
All inputs are finite; a program needn't handle non-finite values.
Results may differ from the reference program's by a relative error of at most 0.015.
Values may be sent and summed in bfloat16 or wider, within the bound.
No kernel may reach another device: no remote copies, remote signals or barrier semaphores. Data moves between devices by JAX's collectives and lax.ppermute only.
A program may use at most 192 MiB of HBM per device.

```python
import math
import jax
import jax.numpy as jnp
import numpy as np
from jax import lax

D = 8192
HA = 512
HB = 52
GROUP = 128
FF = 26624
TOKENS = 16


def field_product(left, right):
    return ((left[0] * right[0] + 2 * left[1] * right[1]) % 5, (left[0] * right[1] + left[1] * right[0]) % 5)


def paley_table():
    members = [(first, second) for first in range(5) for second in range(5)]
    squares = set()
    for member in members:
        if member != (0, 0):
            squares.add(field_product(member, member))
    count = len(members)
    conference = np.zeros((count + 1, count + 1), dtype=np.int64)
    conference[0, 1:] = 1
    conference[1:, 0] = 1
    for row_pos in range(count):
        for col_pos in range(count):
            differ = ((members[row_pos][0] - members[col_pos][0]) % 5, (members[row_pos][1] - members[col_pos][1]) % 5)
            if differ == (0, 0):
                conference[row_pos + 1, col_pos + 1] = 0
            elif differ in squares:
                conference[row_pos + 1, col_pos + 1] = 1
            else:
                conference[row_pos + 1, col_pos + 1] = -1
    plus_block = np.array([[1, 1], [1, -1]], dtype=np.int64)
    zero_block = np.array([[1, -1], [-1, -1]], dtype=np.int64)
    return np.kron(conference, plus_block) + np.kron(np.eye(count + 1, dtype=np.int64), zero_block)


def draw_codes(key, rows_total, cols_total):
    values = jax.random.randint(key, (rows_total, cols_total), -8, 8, dtype=jnp.int32)
    return values.astype(jnp.float32).astype(jnp.bfloat16)


def draw_gate_codes(key, part):
    return draw_codes(jax.random.fold_in(key, 11), D, FF)


def draw_up_codes(key, part):
    return draw_codes(jax.random.fold_in(key, 12), D, FF)


def draw_down_codes(key, part):
    return draw_codes(jax.random.fold_in(key, 13), FF, D)


def draw_hadamard(key, part):
    base = jnp.asarray(paley_table().astype(np.int32))
    row_order = jax.random.permutation(jax.random.fold_in(key, 21), HB)
    col_order = jax.random.permutation(jax.random.fold_in(key, 22), HB)
    row_signs = 2 * jax.random.randint(jax.random.fold_in(key, 23), (HB,), 0, 2, dtype=jnp.int32) - 1
    col_signs = 2 * jax.random.randint(jax.random.fold_in(key, 24), (HB,), 0, 2, dtype=jnp.int32) - 1
    table = base[row_order][:, col_order]
    return (table * row_signs[:, None] * col_signs[None, :]).astype(jnp.int32)


def levels(own_key, extent, pieces, least, top_value):
    loudness = 1.0
    for axis_at, blocks in pieces:
        steps = jax.random.uniform(jax.random.fold_in(jax.random.fold_in(own_key, 6), axis_at), (blocks,), jnp.float32, least / len(pieces), top_value / len(pieces))
        loudness = loudness * jnp.repeat(jnp.exp(steps), extent[axis_at] // blocks).reshape((-1,) + (1,) * (len(extent) - 1 - axis_at))
    return loudness


def gaussian(rng, extent, width, bound, shards=(), kind=jnp.bfloat16):
    result = jax.random.normal(rng, extent, jnp.float32) * width
    if len(shards) > 0:
        result = levels(rng, extent, shards, -0.22, 0.18) * result
    return jnp.clip(result, min=-bound, max=bound).astype(kind)


def setup_inputs(seed: int = 0, part: int = 0) -> dict:
    seeds = jax.random.split(jax.random.key(seed), 9)
    part_splits = jax.random.split(jax.random.fold_in(seeds[8], part), 9)
    tokens = gaussian(part_splits[0], (TOKENS, D), 1.0, 6.0, ((0, 16),))
    gate_codes = draw_gate_codes(jax.random.fold_in(seeds[8], 71), part)
    gate_scales = jnp.clip(jnp.exp(math.log(0.00773398) - 2.3025851 * jax.random.uniform(seeds[2], (D // GROUP, FF), jnp.float32) ** levels(seeds[2], (D // GROUP, FF), ((1, 16),), -0.2, 0.2)), 0.00077339803, 0.00773398)
    up_codes = draw_up_codes(jax.random.fold_in(seeds[8], 71), part)
    up_scales = jnp.clip(jnp.exp(math.log(0.00773398) - 2.3025851 * jax.random.uniform(seeds[4], (D // GROUP, FF), jnp.float32) ** levels(seeds[4], (D // GROUP, FF), ((1, 16),), -0.2, 0.2)), 0.00077339803, 0.00773398)
    down_codes = draw_down_codes(jax.random.fold_in(seeds[8], 71), part)
    down_scales = jnp.clip(jnp.exp(jax.random.uniform(seeds[6], (D,), jnp.float32, math.log(0.00061286293), math.log(0.006128629))), 0.00061286293, 0.006128629)
    hadamard = draw_hadamard(jax.random.fold_in(seeds[8], 71), part)
    return {"tokens": tokens, "gate_codes": gate_codes, "gate_scales": gate_scales, "up_codes": up_codes, "up_scales": up_scales, "down_codes": down_codes, "down_scales": down_scales, "hadamard": hadamard}


def sylvester(size):
    index_vec = jnp.arange(size, dtype=jnp.int32)
    parity = jnp.zeros((size, size), jnp.int32)
    for level in range(max(size.bit_length() - 1, 0)):
        left_bits = jnp.right_shift(index_vec[:, None], level) & 1
        right_bits = jnp.right_shift(index_vec[None, :], level) & 1
        parity = parity + left_bits * right_bits
    return (1 - 2 * (parity % 2)).astype(jnp.float32)

def dequantize(codes, scales):
    row_total, col_total = codes.shape
    group_total = scales.shape[0]
    grouped = codes.astype(jnp.float32).reshape(group_total, row_total // group_total, col_total)
    return (grouped * scales[:, None, :]).reshape(row_total, col_total).astype(jnp.bfloat16)

def reference(tokens, gate_codes, gate_scales, up_codes, up_scales, down_codes, down_scales, hadamard):
    gate_weight = dequantize(gate_codes, gate_scales)
    gate = jnp.dot(tokens, gate_weight, preferred_element_type=jnp.float32)
    up_weight = dequantize(up_codes, up_scales)
    up_part = jnp.dot(tokens, up_weight, preferred_element_type=jnp.float32)
    hidden = jax.nn.silu(gate) * up_part
    cube = hidden.reshape(TOKENS, HA, HB)
    cube = jnp.einsum('tab,ac->tcb', cube, sylvester(HA), precision=lax.Precision.HIGHEST)
    cube = jnp.einsum('tcb,bd->tcd', cube, hadamard.astype(jnp.float32), precision=lax.Precision.HIGHEST)
    rotated = (cube.reshape(TOKENS, FF) * (1.0 / math.sqrt(FF))).astype(jnp.bfloat16)
    summed = jnp.dot(rotated, down_codes, preferred_element_type=jnp.float32)
    return (summed * down_scales[None, :]).astype(jnp.bfloat16)
```

```python
import functools
import math

import jax
import jax.numpy as jnp
from jax import lax
from jax.experimental import pallas as pl
from jax.experimental.pallas import tpu as pltpu
from jax.sharding import PartitionSpec as P

F8 = jnp.float8_e4m3fn
MIB = 2**20
CHUNK = 512
SLOTS = 4


def row_stream(source, buffers, sems, rows):
    total = source.shape[0] // rows
    depth = buffers.shape[0]

    def copy(step):
        slot = lax.rem(step, depth)
        first = pl.multiple_of(step * rows, rows)
        return pltpu.make_async_copy(source.at[pl.ds(first, rows), :], buffers.at[slot], sems.at[slot])

    return total, depth, copy


def pack_kernel(codes_ref, hadamard_ref, packed_ref, turn_ref, buffers, sems):
    total, depth, copy = row_stream(codes_ref, buffers, sems, buffers.shape[1])
    rows = buffers.shape[1]
    for step in range(min(depth, total)):
        copy(step).start()

    size = turn_ref.shape[0]
    small = hadamard_ref.shape[0]
    high = size // small
    unit = lax.broadcasted_iota(jnp.int32, (size, small), 0)
    part = lax.broadcasted_iota(jnp.int32, (size, small), 1)
    pick = (unit % small == part).astype(jnp.bfloat16)
    spread = jnp.dot(pick, hadamard_ref[...].astype(jnp.bfloat16), preferred_element_type=jnp.float32)
    unit_a = lax.broadcasted_iota(jnp.int32, (size, high), 0) // small
    part_a = lax.broadcasted_iota(jnp.int32, (size, high), 1)
    pick_a = (unit_a == part_a).astype(jnp.bfloat16)
    both = unit_a & part_a
    parity = jnp.zeros_like(both)
    for level in range(max(high.bit_length() - 1, 0)):
        parity = parity ^ (jnp.right_shift(both, level) & 1)
    spread_a = (1 - 2 * parity).astype(jnp.bfloat16)
    spread = spread.astype(jnp.bfloat16)
    cols = (((1,), (1,)), ((), ()))
    for first in range(0, size, 128):
        last = min(first + 128, size)
        low = lax.dot_general(spread[first:last], pick, cols, preferred_element_type=jnp.float32)
        top = lax.dot_general(spread_a[first:last], pick_a, cols, preferred_element_type=jnp.float32)
        turn_ref[first:last, :] = (low * top).astype(turn_ref.dtype)

    def body(step, carry):
        slot = lax.rem(step, depth)
        copy(step).wait()
        first = pl.multiple_of(step * rows, rows)
        packed_ref[pl.ds(first, rows), :] = buffers[slot].astype(packed_ref.dtype)

        @pl.when(step + depth < total)
        def _():
            copy(step + depth).start()

        return carry

    lax.fori_loop(0, total, body, 0)


def hidden_kernel(
    group, tokens_ref, gate_ref, gate_scales_ref, up_ref, up_scales_ref, turn_ref, out_ref, buffers, gate_sum, up_sum, sems
):
    total, depth, copy = row_stream(up_ref, buffers, sems, buffers.shape[1])
    rows = buffers.shape[1]
    count = tokens_ref.shape[0]
    for step in range(min(depth, total)):
        copy(step).start()
    gate_sum[...] = jnp.zeros_like(gate_sum)
    up_sum[...] = jnp.zeros_like(up_sum)
    low_half = lax.broadcasted_iota(jnp.int32, (count, 2 * group), 1) < group

    def body(step, carry):
        slot = lax.rem(step, depth)
        copy(step).wait()
        for pair in range(rows // (2 * group)):
            index = step * (rows // (2 * group)) + pair
            first = pl.multiple_of(index * 2 * group, 2 * group)
            two = tokens_ref[:, pl.ds(first, 2 * group)]
            none = jnp.zeros_like(two)
            stacked = jnp.concatenate([jnp.where(low_half, two, none), jnp.where(low_half, none, two)], axis=0)
            gate = jnp.dot(stacked, gate_ref[pl.ds(first, 2 * group), :], preferred_element_type=jnp.float32)
            here = buffers[slot, pair * 2 * group : (pair + 1) * 2 * group, :]
            up = jnp.dot(stacked, here, preferred_element_type=jnp.float32)
            gate_sum[...] += (
                gate[:count] * gate_scales_ref[pl.ds(2 * index, 1), :]
                + gate[count:] * gate_scales_ref[pl.ds(2 * index + 1, 1), :]
            )
            up_sum[...] += (
                up[:count] * up_scales_ref[pl.ds(2 * index, 1), :]
                + up[count:] * up_scales_ref[pl.ds(2 * index + 1, 1), :]
            )

        @pl.when(step + depth < total)
        def _():
            copy(step + depth).start()

        return carry

    lax.fori_loop(0, total, body, 0, unroll=4)
    gate = gate_sum[...]
    hidden = gate / (1.0 + jnp.exp(-gate)) * up_sum[...]
    coarse = hidden.astype(jnp.bfloat16)
    fine = (hidden - coarse.astype(jnp.float32)).astype(jnp.bfloat16)
    both = jnp.dot(jnp.concatenate([coarse, fine], axis=0), turn_ref[...], preferred_element_type=jnp.float32)
    out_ref[...] = both[:count] + both[count:]


def down_kernel(scale, width, turned_ref, codes_ref, out_ref):
    rotated = (turned_ref[...] * scale).astype(jnp.bfloat16)
    for first in range(0, codes_ref.shape[1], width):
        span = slice(first, first + width)
        out_ref[:, span] = jnp.dot(rotated, codes_ref[:, span], preferred_element_type=jnp.float32).astype(out_ref.dtype)


VMEM = pl.BlockSpec(memory_space=pltpu.VMEM)
ANY = pl.BlockSpec(memory_space=pl.ANY)


def in_vmem(value):
    return pltpu.with_memory_space_constraint(value, pltpu.VMEM)


def per_device(
    devices, tokens, gate_codes, gate_scales, up_codes, up_scales, down_codes, down_scales, hadamard
):
    width, units = gate_codes.shape
    group = width // gate_scales.shape[0]
    small = hadamard.shape[0]
    own = tokens.shape[0]
    count = own * devices
    lanes = 128
    total_units = units * devices
    me = lax.axis_index("hx")

    copies = jnp.broadcast_to(tokens.reshape(1, own, width // lanes, lanes), (devices, own, width // lanes, lanes))
    rows = lax.all_to_all(copies, "hx", split_axis=0, concat_axis=0, tiled=True).reshape(count, width)

    gate_packed, turn = pl.pallas_call(
        pack_kernel,
        out_shape=(pltpu.VMEM((width, units), F8), pltpu.VMEM((units, units), F8)),
        in_specs=[ANY, VMEM],
        out_specs=(VMEM, VMEM),
        scratch_shapes=[pltpu.VMEM((SLOTS, CHUNK, units), jnp.bfloat16), pltpu.SemaphoreType.DMA((SLOTS,))],
        compiler_params=pltpu.CompilerParams(vmem_limit_bytes=14 * MIB),
        cost_estimate=pl.CostEstimate(flops=0, bytes_accessed=2 * width * units, transcendentals=0),
    )(gate_codes, hadamard)

    turned = pl.pallas_call(
        functools.partial(hidden_kernel, group),
        out_shape=jax.ShapeDtypeStruct((count, units), jnp.float32),
        in_specs=[VMEM, VMEM, VMEM, ANY, VMEM, VMEM],
        out_specs=VMEM,
        scratch_shapes=[
            pltpu.VMEM((SLOTS, CHUNK, units), jnp.bfloat16),
            pltpu.VMEM((count, units), jnp.float32),
            pltpu.VMEM((count, units), jnp.float32),
            pltpu.SemaphoreType.DMA((SLOTS,)),
        ],
        compiler_params=pltpu.CompilerParams(vmem_limit_bytes=16 * MIB),
        cost_estimate=pl.CostEstimate(flops=4 * count * width * units, bytes_accessed=2 * width * units, transcendentals=0),
    )(rows, in_vmem(gate_packed), gate_scales, up_codes, up_scales, in_vmem(turn))

    bit = 1
    while bit < devices:
        other = lax.ppermute(turned.astype(jnp.bfloat16), "hx", [(at, at ^ bit) for at in range(devices)])
        sign = jnp.where((me & bit) == 0, 1.0, -1.0).astype(jnp.float32)
        turned = turned * sign + other.astype(jnp.float32)
        bit *= 2

    shares = pl.pallas_call(
        functools.partial(down_kernel, 1.0 / math.sqrt(total_units), 1024),
        out_shape=jax.ShapeDtypeStruct((count, width), jnp.bfloat16),
        in_specs=[VMEM, VMEM],
        out_specs=VMEM,
        compiler_params=pltpu.CompilerParams(vmem_limit_bytes=16 * MIB),
        cost_estimate=pl.CostEstimate(flops=2 * count * width * units, bytes_accessed=2 * width * units, transcendentals=0),
    )(turned, in_vmem(down_codes))

    shares = shares.reshape(devices, own, width // lanes, lanes)
    shares = lax.all_to_all(shares, "hx", split_axis=0, concat_axis=0, tiled=True)
    summed = jnp.sum(shares.astype(jnp.float32), axis=0).reshape(own, width)
    return (summed * down_scales[None, :]).astype(jnp.bfloat16)


def solution(mesh):
    in_specs = (
        P(("groups", "hx"), None),
        P(None, "hx"),
        P(None, "hx"),
        P(None, "hx"),
        P(None, "hx"),
        P("hx", None),
        P(),
        P(),
    )
    out_specs = P(("groups", "hx"), None)
    body = functools.partial(per_device, mesh.shape["hx"])
    return jax.shard_map(body, mesh=mesh, in_specs=in_specs, out_specs=out_specs, check_vma=False)
```

```python
import functools
import math

import jax
import jax.numpy as jnp
from jax import lax
from jax.experimental import pallas as pl
from jax.experimental.pallas import tpu as pltpu
from jax.sharding import PartitionSpec as P

MIB = 2**20
LANES = 128
CHUNK = 512
SLOTS = 6
SPAN = 512
AHEAD = 8
SPANS = (5, 3, 3, 5)

VMEM = pl.BlockSpec(memory_space=pltpu.VMEM)
HBM = pl.BlockSpec(memory_space=pltpu.HBM)
ANY = pl.BlockSpec(memory_space=pl.ANY)


def in_vmem(value):
    return pltpu.with_memory_space_constraint(value, pltpu.VMEM)


def in_hbm(value):
    return pltpu.with_memory_space_constraint(value, pltpu.HBM)


def fetch(source, target, sem):
    copy = pltpu.make_async_copy(source, target, sem)
    copy.start()
    return copy


def fetch_columns(first, step, codes_ref, out_ref, sems):
    copies = []
    for index in range(out_ref.shape[1] // step):
        here = codes_ref.at[:, pl.ds(first + index * step, step)]
        copies.append(fetch(here, out_ref.at[:, pl.ds(index * step, step)], sems.at[index]))
    return copies


def columns_kernel(first, step, bit, codes_ref, after_ref, out_ref, sign_ref, sems):
    copies = fetch_columns(first, step, codes_ref, out_ref, sems)
    sign = 1.0 - 2.0 * ((lax.axis_index("hx") // bit) % 2).astype(jnp.float32)
    sign_ref[...] = jnp.full(sign_ref.shape, sign, jnp.float32)
    for copy in copies:
        copy.wait()


def columns_small_kernel(first, step, codes_ref, after_ref, hadamard_ref, out_ref, small_ref, sems):
    copies = [fetch(hadamard_ref, small_ref, sems.at[out_ref.shape[1] // step])]
    copies += fetch_columns(first, step, codes_ref, out_ref, sems)
    for copy in copies:
        copy.wait()


def hidden_kernel(
    group, parts, bits, pieces_ref, gate_codes_ref, gate_scales_ref, up_codes_ref, up_scales_ref,
    gate_ref, up_ref, send_ref, signs_ref, buffers, gate_rows, up_rows, tokens_ref, wide_ref, gate_sum, up_sum, sems, scale_sems,
):
    depth, rows, units = buffers.shape
    everyone, own, tiles, lanes = pieces_ref.shape
    count = everyone // parts * own
    width = tiles * lanes
    steps = width // rows
    mine = lax.axis_index("groups")

    def copy(which, step):
        slot = lax.rem(2 * step + which, depth)
        source = (gate_codes_ref, up_codes_ref)[which]
        first = pl.multiple_of(mine * width + step * rows, rows)
        return pltpu.make_async_copy(source.at[pl.ds(first, rows), :], buffers.at[slot], sems.at[slot])

    first = pl.multiple_of(mine * (width // group), width // group)
    scale_copies = [
        fetch(gate_scales_ref.at[pl.ds(first, width // group), :], gate_rows, scale_sems.at[0]),
        fetch(up_scales_ref.at[pl.ds(first, width // group), :], up_rows, scale_sems.at[1]),
    ]
    ahead = depth // 2
    for step in range(min(ahead, steps)):
        for which in range(2):
            copy(which, step).start()
    me = lax.axis_index("hx")
    for index, bit in enumerate(bits):
        sign = 1.0 - 2.0 * ((me // bit) % 2).astype(jnp.float32)
        signs_ref[index] = jnp.full((count, units), sign, jnp.float32)
    for part in range(parts):
        begin = lax.rem(mine + part, parts) * (everyone // parts)
        for index in range(everyone // parts):
            for at in range(own):
                where = (part * count + index * own + at) * tiles
                wide_ref[where : where + tiles, :] = pieces_ref[begin + index, at].astype(jnp.float32)
    for tile in range(tiles):
        here = wide_ref[pl.ds(tile, parts * count, stride=tiles), :]
        tokens_ref[:, tile * lanes : (tile + 1) * lanes] = here.astype(jnp.bfloat16)
    gate_sum[...] = jnp.zeros_like(gate_sum)
    up_sum[...] = jnp.zeros_like(up_sum)
    low_half = lax.broadcasted_iota(jnp.int32, (parts * count, 2 * group), 1) < group
    for scale_copy in scale_copies:
        scale_copy.wait()

    def add(total_ref, scales_ref, which, step):
        slot = lax.rem(2 * step + which, depth)
        copy(which, step).wait()
        for pair in range(rows // (2 * group)):
            index = step * (rows // (2 * group)) + pair
            two = tokens_ref[:, pl.ds(pl.multiple_of(index * 2 * group, 2 * group), 2 * group)]
            none = jnp.zeros_like(two)
            stacked = jnp.concatenate([jnp.where(low_half, two, none), jnp.where(low_half, none, two)], axis=0)
            codes = buffers[slot, pair * 2 * group : (pair + 1) * 2 * group, :]
            sums = jnp.dot(stacked, codes, preferred_element_type=jnp.float32)
            total_ref[...] += (
                sums[: parts * count] * scales_ref[pl.ds(2 * index, 1), :]
                + sums[parts * count :] * scales_ref[pl.ds(2 * index + 1, 1), :]
            )

        @pl.when(step + ahead < steps)
        def _():
            copy(which, step + ahead).start()

    def body(step, carry):
        add(gate_sum, gate_rows, 0, step)
        add(up_sum, up_rows, 1, step)
        return carry

    lax.fori_loop(0, steps, body, 0, unroll=2)
    gate_ref[...] = gate_sum[:count, :]
    up_ref[...] = up_sum[:count, :]
    for part in range(1, parts):
        span = slice(part * count, (part + 1) * count)
        send_ref[part - 1, 0] = gate_sum[span, :].astype(send_ref.dtype)
        send_ref[part - 1, 1] = up_sum[span, :].astype(send_ref.dtype)


def rotate_kernel(parts, gate_ref, up_ref, hadamard_ref, *refs):
    others = refs[: parts - 1]
    out_ref, send_ref = refs[parts - 1 :]
    count, units = gate_ref.shape
    small = hadamard_ref.shape[0]
    high = units // small
    gate = gate_ref[...]
    up = up_ref[...]
    for other in others:
        gate = gate + other[0].astype(jnp.float32)
        up = up + other[1].astype(jnp.float32)
    hidden = gate / (1.0 + jnp.exp(-gate)) * up
    tall = jnp.concatenate([hidden[:, at * small : (at + 1) * small] for at in range(high)], axis=0)
    coarse = tall.astype(jnp.bfloat16)
    fine = (tall - coarse.astype(jnp.float32)).astype(jnp.bfloat16)
    factor = hadamard_ref[...].astype(jnp.bfloat16)
    tall = jnp.dot(coarse, factor, preferred_element_type=jnp.float32) + jnp.dot(
        fine, factor, preferred_element_type=jnp.float32
    )
    blocks = [tall[at * count : (at + 1) * count] for at in range(high)]
    bit = 1
    while bit < high:
        for at in range(high):
            if at & bit == 0:
                blocks[at], blocks[at | bit] = blocks[at] + blocks[at | bit], blocks[at] - blocks[at | bit]
        bit *= 2
    turned = jnp.concatenate(blocks, axis=1)
    out_ref[...] = turned
    send_ref[...] = turned.astype(send_ref.dtype)


def down_kernel(scale, masks, parts, *refs):
    turned_ref, codes_ref = refs[:2]
    held = refs[2 : 2 + parts]
    keep_ref, send_ref, wide_ref, buffers, sems = refs[2 + parts :]
    depth, _, span = buffers.shape
    begin = sum(part.shape[1] for part in held)
    total = (codes_ref.shape[1] - begin) // span

    def copy(step):
        here = codes_ref.at[:, pl.ds(begin + step * span, span)]
        return pltpu.make_async_copy(here, buffers.at[step % depth], sems.at[step % depth])

    for step in range(min(depth, total)):
        copy(step).start()
    me = lax.axis_index("hx")
    half, own, tiles, lanes = keep_ref.shape
    count = turned_ref.shape[0]
    rotated = (turned_ref[...] * scale).astype(jnp.bfloat16)
    row = lax.broadcasted_iota(jnp.int32, (count, count), 0)
    col = lax.broadcasted_iota(jnp.int32, (count, count), 1)
    slot = row // own
    mask = jnp.zeros_like(slot)
    for index in range(len(masks).bit_length() - 1):
        mask = mask | jnp.where((jnp.right_shift(slot, index) & 1) == 1, masks[1 << index], 0)
    order = ((slot * 0 + me) ^ mask) * own + (row - slot * own) == col
    rotated = jnp.dot(order.astype(jnp.bfloat16), rotated, preferred_element_type=jnp.float32).astype(jnp.bfloat16)

    def put(first, codes):
        sums = jnp.dot(rotated, codes, preferred_element_type=jnp.float32)
        for tile in range(span // lanes):
            wide_ref[pl.ds(first // lanes + tile, count, stride=tiles), :] = sums[:, tile * lanes : (tile + 1) * lanes]

    def put_streamed(step):
        copy(step).wait()
        put(begin + step * span, buffers[step % depth])
        if step + depth < total:
            copy(step + depth).start()

    base = 0
    for part in held:
        for first in range(0, part.shape[1], span):
            put(base + first, part[:, first : first + span])
        base += part.shape[1]
    for step in range(total):
        put_streamed(step)
    for index in range(half):
        for at in range(own):
            first = (index * own + at) * tiles
            keep_ref[index, at] = wide_ref[first : first + tiles, :]
            first += half * own * tiles
            send_ref[index, at] = wide_ref[first : first + tiles, :].astype(send_ref.dtype)


def per_device(
    parts, devices, tokens, gate_codes, gate_scales, up_codes, up_scales, down_codes, down_scales, hadamard
):
    width, units = gate_codes.shape
    group = width // gate_scales.shape[0]
    own = tokens.shape[0]
    count = own * devices
    total_units = units * devices
    bits = [1 << level for level in range(devices.bit_length() - 1)]
    tiles = width // LANES
    share = tiles // parts

    def swap(value, bit):
        return lax.ppermute(value, "hx", [(at, at ^ bit) for at in range(devices)])

    def cost(nbytes, flops=0):
        return pl.CostEstimate(flops=flops, bytes_accessed=nbytes, transcendentals=0)

    pieces = jnp.swapaxes(tokens.reshape(own, parts, share, LANES), 0, 1)
    pieces = jnp.broadcast_to(pieces[:, None], (parts, devices, own, share, LANES))
    pieces = pieces.reshape(parts * devices, own, share, LANES)
    pieces = lax.all_to_all(pieces, ("groups", "hx"), split_axis=0, concat_axis=0, tiled=True)

    early = [bit for index, bit in enumerate(bits) if not 1 <= index < 4]
    gate, up, send, signs = pl.pallas_call(
        functools.partial(hidden_kernel, group, parts, early),
        out_shape=(
            pltpu.VMEM((count, units), jnp.float32),
            pltpu.VMEM((count, units), jnp.float32),
            pltpu.VMEM((parts - 1, 2, count, units), jnp.bfloat16),
            pltpu.VMEM((len(early), count, units), jnp.float32),
        ),
        in_specs=[VMEM, HBM, HBM, HBM, HBM],
        out_specs=(VMEM, VMEM, VMEM, VMEM),
        scratch_shapes=[
            pltpu.VMEM((SLOTS, CHUNK, units), jnp.bfloat16),
            pltpu.VMEM((width // parts // group, units), jnp.float32),
            pltpu.VMEM((width // parts // group, units), jnp.float32),
            pltpu.VMEM((parts * count, width // parts), jnp.bfloat16),
            pltpu.VMEM((parts * count * share, LANES), jnp.float32),
            pltpu.VMEM((parts * count, units), jnp.float32),
            pltpu.VMEM((parts * count, units), jnp.float32),
            pltpu.SemaphoreType.DMA((SLOTS,)),
            pltpu.SemaphoreType.DMA((2,)),
        ],
        compiler_params=pltpu.CompilerParams(vmem_limit_bytes=24 * MIB),
        cost_estimate=cost(4 * width * units // parts, 4 * count * width * units),
    )(pieces, in_hbm(gate_codes), in_hbm(gate_scales), in_hbm(up_codes), in_hbm(up_scales))

    others = [
        lax.ppermute(send[step - 1], "groups", [(at, (at + step) % parts) for at in range(parts)]) for step in range(1, parts)
    ]
    held = []
    first = 0
    columns = SPANS[0] * SPAN
    part, small = pl.pallas_call(
        functools.partial(columns_small_kernel, first, SPAN),
        out_shape=(pltpu.VMEM((units, columns), jnp.bfloat16), pltpu.VMEM(hadamard.shape, hadamard.dtype)),
        in_specs=[HBM, ANY, HBM],
        out_specs=(VMEM, VMEM),
        scratch_shapes=[pltpu.SemaphoreType.DMA((SPANS[0] + 1,))],
        compiler_params=pltpu.CompilerParams(vmem_limit_bytes=2 * MIB),
        cost_estimate=cost(2 * units * columns),
    )(in_hbm(down_codes), send, in_hbm(hadamard))
    held.append(part)
    first += columns

    turned, send = pl.pallas_call(
        functools.partial(rotate_kernel, parts),
        out_shape=(pltpu.VMEM((count, units), jnp.float32), jax.ShapeDtypeStruct((count, units), jnp.bfloat16)),
        in_specs=[VMEM] * (2 + parts),
        out_specs=(VMEM, VMEM),
        compiler_params=pltpu.CompilerParams(vmem_limit_bytes=8 * MIB),
        cost_estimate=cost(16 * count * units),
    )(in_vmem(gate), in_vmem(up), in_vmem(small), *others)

    for index, bit in enumerate(bits):
        other = swap(send, bit)
        if 1 <= index < 4:
            columns = SPANS[index] * SPAN
            part, sign = pl.pallas_call(
                functools.partial(columns_kernel, first, SPAN, bit),
                out_shape=(pltpu.VMEM((units, columns), jnp.bfloat16), pltpu.VMEM((count, units), jnp.float32)),
                in_specs=[HBM, ANY],
                out_specs=(VMEM, VMEM),
                scratch_shapes=[pltpu.SemaphoreType.DMA((SPANS[index],))],
                compiler_params=pltpu.CompilerParams(vmem_limit_bytes=2 * MIB),
                cost_estimate=cost(2 * units * columns),
            )(in_hbm(down_codes), send)
            held.append(part)
            first += columns
        else:
            sign = signs[early.index(bit)]
        turned = turned * sign + other.astype(jnp.float32)
        send = turned.astype(jnp.bfloat16)

    order = [1] + [bit for bit in bits[1:]]
    spread = [0]
    for bit in reversed(order):
        spread = spread + [mask | bit for mask in spread]
    ahead = max(min((width - first) // SPAN, AHEAD), 1)
    keep, send = pl.pallas_call(
        functools.partial(down_kernel, 1.0 / math.sqrt(total_units), spread, len(held)),
        out_shape=(
            jax.ShapeDtypeStruct((devices // 2, own, tiles, LANES), jnp.float32),
            jax.ShapeDtypeStruct((devices // 2, own, tiles, LANES), jnp.bfloat16),
        ),
        in_specs=[VMEM, HBM] + [VMEM] * len(held),
        out_specs=(VMEM, VMEM),
        scratch_shapes=[
            pltpu.VMEM((count * tiles, LANES), jnp.float32),
            pltpu.VMEM((ahead, units, SPAN), jnp.bfloat16),
            pltpu.SemaphoreType.DMA((ahead,)),
        ],
        compiler_params=pltpu.CompilerParams(vmem_limit_bytes=20 * MIB),
        cost_estimate=cost(width * units, 2 * count * width * units),
    )(turned, in_hbm(down_codes), *[in_vmem(part) for part in held])
    summed = keep + swap(send, order[0]).astype(jnp.float32)
    for bit in order[1:]:
        half = summed.shape[0] // 2
        summed = summed[:half] + swap(summed[half:].astype(jnp.bfloat16), bit).astype(jnp.float32)
    return (summed.reshape(own, width) * down_scales[None, :]).astype(jnp.bfloat16)


def solution(mesh):
    in_specs = (
        P(("groups", "hx"), None),
        P(None, "hx"),
        P(None, "hx"),
        P(None, "hx"),
        P(None, "hx"),
        P("hx", None),
        P(),
        P(),
    )
    out_specs = P(("groups", "hx"), None)
    body = functools.partial(per_device, mesh.shape["groups"], mesh.shape["hx"])
    return jax.shard_map(body, mesh=mesh, in_specs=in_specs, out_specs=out_specs, check_vma=False)
```

```python
import functools
import math

import jax
import jax.numpy as jnp
from jax import lax
from jax.experimental import pallas as pl
from jax.experimental.pallas import tpu as pltpu
from jax.sharding import PartitionSpec as P

MIB = 2**20
F8 = jnp.float8_e4m3fn
LANES = 128
CHUNK = 512
SLOTS = 5
UNROLL = 2
ROWS = (2, 5, 5)
SPAN = 512
AHEAD = 8
SPANS = (0, 5, 5, 6)

VMEM = pl.BlockSpec(memory_space=pltpu.VMEM)
HBM = pl.BlockSpec(memory_space=pltpu.HBM)
ANY = pl.BlockSpec(memory_space=pl.ANY)


def in_vmem(value):
    return pltpu.with_memory_space_constraint(value, pltpu.VMEM)


def in_hbm(value):
    return pltpu.with_memory_space_constraint(value, pltpu.HBM)


def fetch(source, target, sem):
    copy = pltpu.make_async_copy(source, target, sem)
    copy.start()
    return copy


def fetch_columns(first, step, codes_ref, out_ref, sems):
    copies = []
    for index in range(out_ref.shape[1] // step):
        here = codes_ref.at[:, pl.ds(first + index * step, step)]
        copies.append(fetch(here, out_ref.at[:, pl.ds(index * step, step)], sems.at[index]))
    return copies


def columns_kernel(first, step, bit, codes_ref, after_ref, out_ref, sign_ref, sems):
    copies = fetch_columns(first, step, codes_ref, out_ref, sems)
    sign = 1.0 - 2.0 * ((lax.axis_index("hx") // bit) % 2).astype(jnp.float32)
    sign_ref[...] = jnp.full(sign_ref.shape, sign, jnp.float32)
    for copy in copies:
        copy.wait()


def rows_kernel(first, step, codes_ref, after_ref, out_ref, same_ref, sems):
    copies = [fetch(after_ref, same_ref, sems.at[out_ref.shape[0] // step])]
    for index in range(out_ref.shape[0] // step):
        here = codes_ref.at[pl.ds(first + index * step, step), :]
        copies.append(fetch(here, out_ref.at[pl.ds(index * step, step), :], sems.at[index]))
    for copy in copies:
        copy.wait()


def first_rows_kernel(first, step, codes_ref, tokens_ref, out_ref, tiled_ref, token_ref, wide_ref, sems):
    _, own, tiles, lanes = tiled_ref.shape
    token = fetch(tokens_ref, token_ref, sems.at[out_ref.shape[0] // step])
    copies = []
    for index in range(out_ref.shape[0] // step):
        here = codes_ref.at[pl.ds(first + index * step, step), :]
        copies.append(fetch(here, out_ref.at[pl.ds(index * step, step), :], sems.at[index]))
    token.wait()
    for at in range(own):
        row = token_ref[at : at + 1, :].astype(jnp.float32)
        for tile in range(tiles):
            wide_ref[tile : tile + 1, :] = row[:, tile * lanes : (tile + 1) * lanes]
        tiled_ref[0, at] = wide_ref[...].astype(tiled_ref.dtype)
    for copy in copies:
        copy.wait()


def rotate(gate, up, hadamard):
    count, units = gate.shape
    small = hadamard.shape[0]
    high = units // small
    hidden = gate / (1.0 + jnp.exp(-gate)) * up
    tall = jnp.concatenate([hidden[:, at * small : (at + 1) * small] for at in range(high)], axis=0)
    coarse = tall.astype(jnp.bfloat16)
    fine = (tall - coarse.astype(jnp.float32)).astype(jnp.bfloat16)
    factor = hadamard.astype(jnp.bfloat16)
    tall = jnp.dot(coarse, factor, preferred_element_type=jnp.float32) + jnp.dot(
        fine, factor, preferred_element_type=jnp.float32
    )
    blocks = [tall[at * count : (at + 1) * count] for at in range(high)]
    bit = 1
    while bit < high:
        for at in range(high):
            if at & bit == 0:
                blocks[at], blocks[at | bit] = blocks[at] + blocks[at | bit], blocks[at] - blocks[at | bit]
        bit *= 2
    return jnp.concatenate(blocks, axis=1)


def hidden_kernel(group, masks, bits, parts, *refs):
    pieces_ref, gate_codes_ref, gate_scales_ref, up_codes_ref, up_scales_ref, hadamard_ref = refs[:6]
    held = refs[6 : 6 + parts]
    out_ref, send_ref, signs_ref, buffers, late, gate_rows, up_rows, small_ref, tokens_ref, wide_ref = refs[6 + parts : 16 + parts]
    gate_sum, up_sum, sems, late_sems, small_sems = refs[16 + parts :]
    depth, rows, units = buffers.shape
    devices, own, tiles, lanes = pieces_ref.shape
    count = devices * own
    steps = up_codes_ref.shape[0] // rows
    ready = sum(part.shape[0] for part in held) // rows
    late_steps = steps - ready

    def copy(step):
        slot = lax.rem(step, depth)
        first = pl.multiple_of(step * rows, rows)
        return pltpu.make_async_copy(up_codes_ref.at[pl.ds(first, rows), :], buffers.at[slot], sems.at[slot])

    def late_copy(index):
        source = gate_codes_ref.at[pl.ds(pl.multiple_of((ready + index) * rows, rows), rows), :]
        target = late.at[pl.ds(pl.multiple_of(index * rows, rows), rows), :]
        return pltpu.make_async_copy(source, target, late_sems.at[index])

    copy(0).start()
    small_copies = [
        fetch(up_scales_ref, up_rows, small_sems.at[1]),
        fetch(gate_scales_ref, gate_rows, small_sems.at[0]),
        fetch(hadamard_ref, small_ref, small_sems.at[2]),
    ]
    for step in range(1, min(depth, steps)):
        copy(step).start()
    me = lax.axis_index("hx")
    for index, bit in enumerate(bits):
        sign = 1.0 - 2.0 * ((me // bit) % 2).astype(jnp.float32)
        signs_ref[index] = jnp.full((count, units), sign, jnp.float32)
    for slot, mask in enumerate(masks):
        for at in range(own):
            where = pl.multiple_of(((me ^ mask) * own + at) * tiles, tiles)
            wide_ref[pl.ds(where, tiles), :] = pieces_ref[slot, at].astype(jnp.float32)
    for tile in range(tiles):
        here = wide_ref[pl.ds(tile, count, stride=tiles), :]
        tokens_ref[:, tile * lanes : (tile + 1) * lanes] = here.astype(jnp.bfloat16)
    gate_sum[...] = jnp.zeros_like(gate_sum)
    up_sum[...] = jnp.zeros_like(up_sum)
    low_half = lax.broadcasted_iota(jnp.int32, (count, 2 * group), 1) < group
    for small_copy in small_copies:
        small_copy.wait()

    def add(total_ref, scales_ref, step, codes):
        for pair in range(rows // (2 * group)):
            index = step * (rows // (2 * group)) + pair
            two = tokens_ref[:, pl.ds(pl.multiple_of(index * 2 * group, 2 * group), 2 * group)]
            none = jnp.zeros_like(two)
            stacked = jnp.concatenate([jnp.where(low_half, two, none), jnp.where(low_half, none, two)], axis=0)
            sums = jnp.dot(stacked, codes(pair * 2 * group).astype(F8), preferred_element_type=jnp.float32)
            total_ref[...] += (
                sums[:count] * scales_ref[pl.ds(2 * index, 1), :] + sums[count:] * scales_ref[pl.ds(2 * index + 1, 1), :]
            )

    def loop(begin, end, source, base, waits):
        def body(step, carry):
            slot = lax.rem(step, depth)

            def in_source(first):
                return source[pl.ds(pl.multiple_of((step - base) * rows + first, 2 * group), 2 * group), :]

            def in_buffer(first):
                return buffers[slot, first : first + 2 * group, :]

            if not waits:

                @pl.when((lax.rem(step, 2) == 0) & (step // 2 < late_steps))
                def _():
                    late_copy(step // 2).start()

            else:
                late_copy(step - ready).wait()
            add(gate_sum, gate_rows, step, in_source)
            copy(step).wait()
            add(up_sum, up_rows, step, in_buffer)

            @pl.when(step + depth < steps)
            def _():
                copy(step + depth).start()

            return carry

        lax.fori_loop(begin, end, body, 0, unroll=UNROLL)

    before = 0
    for part in held:
        here = part.shape[0] // rows
        loop(before, before + here, part, before, False)
        before += here
    for index in range((ready + 1) // 2, late_steps):
        late_copy(index).start()
    loop(ready, steps, late, ready, True)
    turned = rotate(gate_sum[...], up_sum[...], small_ref[...])
    out_ref[...] = turned
    send_ref[...] = turned.astype(send_ref.dtype)


def down_kernel(scale, masks, parts, *refs):
    turned_ref, codes_ref = refs[:2]
    held = refs[2 : 2 + parts]
    keep_ref, send_ref, wide_ref, buffers, sems = refs[2 + parts :]
    depth, _, span = buffers.shape
    begin = sum(part.shape[1] for part in held)
    total = (codes_ref.shape[1] - begin) // span

    def copy(step):
        here = codes_ref.at[:, pl.ds(begin + step * span, span)]
        return pltpu.make_async_copy(here, buffers.at[step % depth], sems.at[step % depth])

    for step in range(min(depth, total)):
        copy(step).start()
    me = lax.axis_index("hx")
    half, own, tiles, lanes = keep_ref.shape
    count = turned_ref.shape[0]
    rotated = (turned_ref[...] * scale).astype(jnp.bfloat16)
    row = lax.broadcasted_iota(jnp.int32, (count, count), 0)
    col = lax.broadcasted_iota(jnp.int32, (count, count), 1)
    slot = row // own
    mask = jnp.zeros_like(slot)
    for index in range(len(masks).bit_length() - 1):
        mask = mask | jnp.where((jnp.right_shift(slot, index) & 1) == 1, masks[1 << index], 0)
    order = ((slot * 0 + me) ^ mask) * own + (row - slot * own) == col
    rotated = jnp.dot(order.astype(jnp.bfloat16), rotated, preferred_element_type=jnp.float32).astype(jnp.bfloat16)

    def put(first, codes):
        sums = jnp.dot(rotated, codes.astype(F8), preferred_element_type=jnp.float32)
        for tile in range(span // lanes):
            wide_ref[pl.ds(first // lanes + tile, count, stride=tiles), :] = sums[:, tile * lanes : (tile + 1) * lanes]

    def put_streamed(step):
        copy(step).wait()
        put(begin + step * span, buffers[step % depth])
        if step + depth < total:
            copy(step + depth).start()

    base = 0
    for part in held:
        for first in range(0, part.shape[1], span):
            put(base + first, part[:, first : first + span])
        base += part.shape[1]
    for step in range(total):
        put_streamed(step)
    for index in range(half):
        for at in range(own):
            first = (index * own + at) * tiles
            keep_ref[index, at] = wide_ref[first : first + tiles, :]
            first += half * own * tiles
            send_ref[index, at] = wide_ref[first : first + tiles, :].astype(send_ref.dtype)


def per_device(
    devices, tokens, gate_codes, gate_scales, up_codes, up_scales, down_codes, down_scales, hadamard
):
    width, units = gate_codes.shape
    group = width // gate_scales.shape[0]
    own = tokens.shape[0]
    count = own * devices
    total_units = units * devices
    bits = [1 << level for level in range(devices.bit_length() - 1)]
    tiles = width // LANES

    def swap(value, bit):
        return lax.ppermute(value, "hx", [(at, at ^ bit) for at in range(devices)])

    def cost(nbytes, flops=0):
        return pl.CostEstimate(flops=flops, bytes_accessed=nbytes, transcendentals=0)

    pieces = tokens
    gathered = [0]
    held = []
    first = 0
    for index, bit in enumerate(reversed(bits)):
        other = swap(pieces, bit)
        if index < len(ROWS):
            rows = ROWS[index] * CHUNK
            scratch = [pltpu.SemaphoreType.DMA((ROWS[index] + 1,))]
            if index == 0:
                scratch = [pltpu.VMEM((own, width), tokens.dtype), pltpu.VMEM((tiles, LANES), jnp.float32)] + scratch
            part, pieces = pl.pallas_call(
                functools.partial(first_rows_kernel if index == 0 else rows_kernel, first, CHUNK),
                out_shape=(
                    pltpu.VMEM((rows, units), jnp.bfloat16),
                    pltpu.VMEM((1 << index, own, tiles, LANES), tokens.dtype),
                ),
                in_specs=[HBM, HBM if index == 0 else ANY],
                out_specs=(VMEM, VMEM),
                scratch_shapes=scratch,
                compiler_params=pltpu.CompilerParams(vmem_limit_bytes=2 * MIB),
                cost_estimate=cost(2 * rows * units),
            )(in_hbm(gate_codes), in_hbm(pieces) if index == 0 else pieces)
            held.append(part)
            first += rows
        if index == 0:
            other = other.reshape(1, own, tiles, LANES)
        pieces = jnp.concatenate([pieces, other], axis=0)
        gathered = gathered + [mask | bit for mask in gathered]

    early = [bit for index, bit in enumerate(bits) if not 1 <= index < 4]
    turned, send, signs = pl.pallas_call(
        functools.partial(hidden_kernel, group, gathered, early, len(held)),
        out_shape=(
            pltpu.VMEM((count, units), jnp.float32),
            jax.ShapeDtypeStruct((count, units), jnp.bfloat16),
            pltpu.VMEM((len(early), count, units), jnp.float32),
        ),
        in_specs=[VMEM, HBM, HBM, HBM, HBM, HBM] + [VMEM] * len(held),
        out_specs=(VMEM, VMEM, VMEM),
        scratch_shapes=[
            pltpu.VMEM((SLOTS, CHUNK, units), jnp.bfloat16),
            pltpu.VMEM((width - first, units), jnp.bfloat16),
            pltpu.VMEM(gate_scales.shape, gate_scales.dtype),
            pltpu.VMEM(up_scales.shape, up_scales.dtype),
            pltpu.VMEM(hadamard.shape, hadamard.dtype),
            pltpu.VMEM((count, width), jnp.bfloat16),
            pltpu.VMEM((count * tiles, LANES), jnp.float32),
            pltpu.VMEM((count, units), jnp.float32),
            pltpu.VMEM((count, units), jnp.float32),
            pltpu.SemaphoreType.DMA((SLOTS,)),
            pltpu.SemaphoreType.DMA(((width - first) // CHUNK,)),
            pltpu.SemaphoreType.DMA((3,)),
        ],
        compiler_params=pltpu.CompilerParams(vmem_limit_bytes=28 * MIB),
        cost_estimate=cost(4 * width * units, 4 * count * width * units),
    )(
        pieces, in_hbm(gate_codes), in_hbm(gate_scales), in_hbm(up_codes), in_hbm(up_scales), in_hbm(hadamard),
        *[in_vmem(part) for part in held],
    )
    held = []
    first = 0

    for index, bit in enumerate(bits):
        other = swap(send, bit)
        if 1 <= index < 4:
            columns = SPANS[index] * SPAN
            part, sign = pl.pallas_call(
                functools.partial(columns_kernel, first, SPAN, bit),
                out_shape=(pltpu.VMEM((units, columns), jnp.bfloat16), pltpu.VMEM((count, units), jnp.float32)),
                in_specs=[HBM, ANY],
                out_specs=(VMEM, VMEM),
                scratch_shapes=[pltpu.SemaphoreType.DMA((SPANS[index],))],
                compiler_params=pltpu.CompilerParams(vmem_limit_bytes=2 * MIB),
                cost_estimate=cost(2 * units * columns),
            )(in_hbm(down_codes), send)
            held.append(part)
            first += columns
        else:
            sign = signs[early.index(bit)]
        turned = turned * sign + other.astype(jnp.float32)
        send = turned.astype(jnp.bfloat16)

    order = [1] + [bit for bit in bits[1:]]
    spread = [0]
    for bit in reversed(order):
        spread = spread + [mask | bit for mask in spread]
    ahead = max(min((width - first) // SPAN, AHEAD), 1)
    keep, send = pl.pallas_call(
        functools.partial(down_kernel, 1.0 / math.sqrt(total_units), spread, len(held)),
        out_shape=(
            jax.ShapeDtypeStruct((devices // 2, own, tiles, LANES), jnp.float32),
            jax.ShapeDtypeStruct((devices // 2, own, tiles, LANES), jnp.bfloat16),
        ),
        in_specs=[VMEM, HBM] + [VMEM] * len(held),
        out_specs=(VMEM, VMEM),
        scratch_shapes=[
            pltpu.VMEM((count * tiles, LANES), jnp.float32),
            pltpu.VMEM((ahead, units, SPAN), jnp.bfloat16),
            pltpu.SemaphoreType.DMA((ahead,)),
        ],
        compiler_params=pltpu.CompilerParams(vmem_limit_bytes=20 * MIB),
        cost_estimate=cost(width * units, 2 * count * width * units),
    )(turned, in_hbm(down_codes), *[in_vmem(part) for part in held])
    summed = keep + swap(send, order[0]).astype(jnp.float32)
    for bit in order[1:]:
        half = summed.shape[0] // 2
        summed = summed[:half] + swap(summed[half:].astype(jnp.bfloat16), bit).astype(jnp.float32)
    return (summed.reshape(own, width) * down_scales[None, :]).astype(jnp.bfloat16)


def solution(mesh):
    in_specs = (
        P(("groups", "hx"), None),
        P(None, "hx"),
        P(None, "hx"),
        P(None, "hx"),
        P(None, "hx"),
        P("hx", None),
        P(),
        P(),
    )
    out_specs = P(("groups", "hx"), None)
    body = functools.partial(per_device, mesh.shape["hx"])
    return jax.shard_map(body, mesh=mesh, in_specs=in_specs, out_specs=out_specs, check_vma=False)
```

```python
import functools
import math

import jax
import jax.numpy as jnp
from jax import lax
from jax.experimental import pallas as pl
from jax.experimental.pallas import tpu as pltpu
from jax.sharding import PartitionSpec as P

MIB = 2**20
F8 = jnp.float8_e4m3fn
LANES = 128
CHUNK = 512
SLOTS = 5
UNROLL = 2
ROWS = (2, 2, 2, 2)
SPAN = 512
AHEAD = 8
SPANS = (5, 3, 3, 5)

VMEM = pl.BlockSpec(memory_space=pltpu.VMEM)
HBM = pl.BlockSpec(memory_space=pltpu.HBM)
ANY = pl.BlockSpec(memory_space=pl.ANY)


def in_vmem(value):
    return pltpu.with_memory_space_constraint(value, pltpu.VMEM)


def in_hbm(value):
    return pltpu.with_memory_space_constraint(value, pltpu.HBM)


def fetch(source, target, sem):
    copy = pltpu.make_async_copy(source, target, sem)
    copy.start()
    return copy


def fetch_columns(first, step, codes_ref, out_ref, sems):
    copies = []
    for index in range(out_ref.shape[1] // step):
        here = codes_ref.at[:, pl.ds(first + index * step, step)]
        copies.append(fetch(here, out_ref.at[:, pl.ds(index * step, step)], sems.at[index]))
    return copies


def columns_kernel(first, step, bit, codes_ref, after_ref, out_ref, sign_ref, sems):
    copies = fetch_columns(first, step, codes_ref, out_ref, sems)
    sign = 1.0 - 2.0 * ((lax.axis_index("hx") // bit) % 2).astype(jnp.float32)
    sign_ref[...] = jnp.full(sign_ref.shape, sign, jnp.float32)
    for copy in copies:
        copy.wait()


def rows_kernel(before, step, codes_ref, after_ref, out_ref, same_ref, sems):
    copies = [fetch(after_ref, same_ref, sems.at[out_ref.shape[0] // step])]
    share = codes_ref.shape[0] // lax.axis_size("groups")
    first = pl.multiple_of(lax.axis_index("groups") * share + before, step)
    for index in range(out_ref.shape[0] // step):
        here = codes_ref.at[pl.ds(first + index * step, step), :]
        copies.append(fetch(here, out_ref.at[pl.ds(index * step, step), :], sems.at[index]))
    for copy in copies:
        copy.wait()


def columns_small_kernel(first, step, codes_ref, after_ref, hadamard_ref, out_ref, small_ref, sems):
    copies = [fetch(hadamard_ref, small_ref, sems.at[out_ref.shape[1] // step])]
    copies += fetch_columns(first, step, codes_ref, out_ref, sems)
    for copy in copies:
        copy.wait()


def tiles_kernel(mine_ref, *refs):
    others, out_ref, wide_ref = refs[:-2], refs[-2], refs[-1]
    _, own, tiles, lanes = out_ref.shape
    first = pl.multiple_of(lax.axis_index("groups") * (tiles * lanes), tiles * lanes)
    for index, token_ref in enumerate((mine_ref,) + others):
        for at in range(own):
            row = token_ref[at : at + 1, pl.ds(first, tiles * lanes)].astype(jnp.float32)
            for tile in range(tiles):
                wide_ref[tile : tile + 1, :] = row[:, tile * lanes : (tile + 1) * lanes]
            out_ref[index, at] = wide_ref[...].astype(out_ref.dtype)


def rotate(gate, up, hadamard):
    count, units = gate.shape
    small = hadamard.shape[0]
    high = units // small
    hidden = gate / (1.0 + jnp.exp(-gate)) * up
    tall = jnp.concatenate([hidden[:, at * small : (at + 1) * small] for at in range(high)], axis=0)
    coarse = tall.astype(jnp.bfloat16)
    fine = (tall - coarse.astype(jnp.float32)).astype(jnp.bfloat16)
    factor = hadamard.astype(jnp.bfloat16)
    tall = jnp.dot(coarse, factor, preferred_element_type=jnp.float32) + jnp.dot(
        fine, factor, preferred_element_type=jnp.float32
    )
    blocks = [tall[at * count : (at + 1) * count] for at in range(high)]
    bit = 1
    while bit < high:
        for at in range(high):
            if at & bit == 0:
                blocks[at], blocks[at | bit] = blocks[at] + blocks[at | bit], blocks[at] - blocks[at | bit]
        bit *= 2
    return jnp.concatenate(blocks, axis=1)


def rotate_kernel(gate_ref, up_ref, hadamard_ref, *refs):
    others, out_ref, send_ref = refs[:-2], refs[-2], refs[-1]
    gate = gate_ref[...]
    up = up_ref[...]
    for other in others:
        gate = gate + other[0].astype(jnp.float32)
        up = up + other[1].astype(jnp.float32)
    turned = rotate(gate, up, hadamard_ref[...])
    out_ref[...] = turned
    send_ref[...] = turned.astype(send_ref.dtype)


def hidden_kernel(group, parts, masks, bits, *refs):
    pieces_ref, gate_scales_ref, up_codes_ref, up_scales_ref = refs[:4]
    held = refs[4:-12]
    gate_ref, up_ref, send_ref, signs_ref, buffers, gate_rows, up_rows, tokens_ref, wide_ref, gate_sum, up_sum, sems = refs[-12:]
    depth, rows, units = buffers.shape
    slots, own, tiles, lanes = pieces_ref.shape
    count = slots // parts * own
    share = tiles * lanes
    steps = share // rows
    mine = lax.axis_index("groups")

    def copy(step):
        slot = lax.rem(step, depth)
        first = pl.multiple_of(mine * share + step * rows, rows)
        return pltpu.make_async_copy(up_codes_ref.at[pl.ds(first, rows), :], buffers.at[slot], sems.at[slot])

    first = pl.multiple_of(mine * (share // group), share // group)
    small_copies = [
        fetch(gate_scales_ref.at[pl.ds(first, share // group), :], gate_rows, sems.at[depth]),
        fetch(up_scales_ref.at[pl.ds(first, share // group), :], up_rows, sems.at[depth + 1]),
    ]
    for step in range(min(depth, steps)):
        copy(step).start()
    me = lax.axis_index("hx")
    for index, bit in enumerate(bits):
        sign = 1.0 - 2.0 * ((me // bit) % 2).astype(jnp.float32)
        signs_ref[index] = jnp.full((count, units), sign, jnp.float32)
    for slot, mask in enumerate(masks):
        for part in range(parts):
            for at in range(own):
                where = pl.multiple_of((part * count + (me ^ mask) * own + at) * tiles, tiles)
                wide_ref[pl.ds(where, tiles), :] = pieces_ref[slot * parts + part, at].astype(jnp.float32)
    for tile in range(tiles):
        here = wide_ref[pl.ds(tile, parts * count, stride=tiles), :]
        tokens_ref[:, tile * lanes : (tile + 1) * lanes] = here.astype(jnp.bfloat16)
    gate_sum[...] = jnp.zeros_like(gate_sum)
    up_sum[...] = jnp.zeros_like(up_sum)
    low_half = lax.broadcasted_iota(jnp.int32, (parts * count, 2 * group), 1) < group
    for small_copy in small_copies:
        small_copy.wait()

    def add(total_ref, scales_ref, step, codes):
        for pair in range(rows // (2 * group)):
            index = step * (rows // (2 * group)) + pair
            two = tokens_ref[:, pl.ds(pl.multiple_of(index * 2 * group, 2 * group), 2 * group)]
            none = jnp.zeros_like(two)
            stacked = jnp.concatenate([jnp.where(low_half, two, none), jnp.where(low_half, none, two)], axis=0)
            sums = jnp.dot(stacked, codes(pair * 2 * group).astype(F8), preferred_element_type=jnp.float32)
            total_ref[...] += (
                sums[: parts * count] * scales_ref[pl.ds(2 * index, 1), :]
                + sums[parts * count :] * scales_ref[pl.ds(2 * index + 1, 1), :]
            )

    before = 0
    for part in held:

        def body(step, carry, part=part, before=before):
            slot = lax.rem(step, depth)

            def in_part(first):
                return part[pl.ds(pl.multiple_of((step - before) * rows + first, 2 * group), 2 * group), :]

            def in_buffer(first):
                return buffers[slot, first : first + 2 * group, :]

            add(gate_sum, gate_rows, step, in_part)
            copy(step).wait()
            add(up_sum, up_rows, step, in_buffer)

            @pl.when(step + depth < steps)
            def _():
                copy(step + depth).start()

            return carry

        lax.fori_loop(before, before + part.shape[0] // rows, body, 0, unroll=UNROLL)
        before += part.shape[0] // rows
    gate_ref[...] = gate_sum[:count, :]
    up_ref[...] = up_sum[:count, :]
    for part in range(1, parts):
        span = slice(part * count, (part + 1) * count)
        send_ref[part - 1, 0] = gate_sum[span, :].astype(send_ref.dtype)
        send_ref[part - 1, 1] = up_sum[span, :].astype(send_ref.dtype)


def down_kernel(scale, masks, parts, *refs):
    turned_ref, codes_ref = refs[:2]
    held = refs[2 : 2 + parts]
    keep_ref, send_ref, wide_ref, buffers, sems = refs[2 + parts :]
    depth, _, span = buffers.shape
    begin = sum(part.shape[1] for part in held)
    total = (codes_ref.shape[1] - begin) // span

    def copy(step):
        here = codes_ref.at[:, pl.ds(begin + step * span, span)]
        return pltpu.make_async_copy(here, buffers.at[step % depth], sems.at[step % depth])

    for step in range(min(depth, total)):
        copy(step).start()
    me = lax.axis_index("hx")
    half, own, tiles, lanes = keep_ref.shape
    count = turned_ref.shape[0]
    rotated = (turned_ref[...] * scale).astype(jnp.bfloat16)
    row = lax.broadcasted_iota(jnp.int32, (count, count), 0)
    col = lax.broadcasted_iota(jnp.int32, (count, count), 1)
    slot = row // own
    mask = jnp.zeros_like(slot)
    for index in range(len(masks).bit_length() - 1):
        mask = mask | jnp.where((jnp.right_shift(slot, index) & 1) == 1, masks[1 << index], 0)
    order = ((slot * 0 + me) ^ mask) * own + (row - slot * own) == col
    rotated = jnp.dot(order.astype(jnp.bfloat16), rotated, preferred_element_type=jnp.float32).astype(jnp.bfloat16)

    def put(first, codes):
        sums = jnp.dot(rotated, codes.astype(F8), preferred_element_type=jnp.float32)
        for tile in range(span // lanes):
            wide_ref[pl.ds(first // lanes + tile, count, stride=tiles), :] = sums[:, tile * lanes : (tile + 1) * lanes]

    def put_streamed(step):
        copy(step).wait()
        put(begin + step * span, buffers[step % depth])
        if step + depth < total:
            copy(step + depth).start()

    base = 0
    for part in held:
        for first in range(0, part.shape[1], span):
            put(base + first, part[:, first : first + span])
        base += part.shape[1]
    for step in range(total):
        put_streamed(step)
    for index in range(half):
        for at in range(own):
            first = (index * own + at) * tiles
            keep_ref[index, at] = wide_ref[first : first + tiles, :]
            first += half * own * tiles
            send_ref[index, at] = wide_ref[first : first + tiles, :].astype(send_ref.dtype)


def per_device(
    parts, devices, tokens, gate_codes, gate_scales, up_codes, up_scales, down_codes, down_scales, hadamard
):
    width, units = gate_codes.shape
    group = width // gate_scales.shape[0]
    own = tokens.shape[0]
    count = own * devices
    total_units = units * devices
    bits = [1 << level for level in range(devices.bit_length() - 1)]
    tiles = width // LANES

    def swap(value, bit):
        return lax.ppermute(value, "hx", [(at, at ^ bit) for at in range(devices)])

    def cost(nbytes, flops=0):
        return pl.CostEstimate(flops=flops, bytes_accessed=nbytes, transcendentals=0)

    share = width // parts
    tiles_here = tiles // parts

    def by_part(value, step):
        return lax.ppermute(value, "groups", [(at, (at + step) % parts) for at in range(parts)])

    def some_rows(index, first, after, in_space):
        rows = ROWS[index] * CHUNK
        return pl.pallas_call(
            functools.partial(rows_kernel, first, CHUNK),
            out_shape=(pltpu.VMEM((rows, units), jnp.bfloat16), pltpu.VMEM(after.shape, after.dtype)),
            in_specs=[HBM, in_space],
            out_specs=(VMEM, VMEM),
            scratch_shapes=[pltpu.SemaphoreType.DMA((ROWS[index] + 1,))],
            compiler_params=pltpu.CompilerParams(vmem_limit_bytes=2 * MIB),
            cost_estimate=cost(2 * rows * units),
        )(in_hbm(gate_codes), after)

    others = [by_part(tokens, step) for step in range(1, parts)]
    part, mine = some_rows(0, 0, in_hbm(tokens), HBM)
    held = [part]
    first = part.shape[0]
    pieces = pl.pallas_call(
        tiles_kernel,
        out_shape=jax.ShapeDtypeStruct((parts, own, tiles_here, LANES), tokens.dtype),
        in_specs=[VMEM] * parts,
        out_specs=VMEM,
        scratch_shapes=[pltpu.VMEM((tiles_here, LANES), jnp.float32)],
        compiler_params=pltpu.CompilerParams(vmem_limit_bytes=2 * MIB),
        cost_estimate=cost(4 * own * width),
    )(in_vmem(mine), *others)
    gathered = [0]
    for index, bit in enumerate(reversed(bits)):
        other = swap(pieces, bit)
        if index + 1 < len(ROWS):
            part, pieces = some_rows(index + 1, first, pieces, ANY)
            held.append(part)
            first += part.shape[0]
        pieces = jnp.concatenate([pieces, other], axis=0)
        gathered = gathered + [mask | bit for mask in gathered]

    early = [bit for index, bit in enumerate(bits) if not 1 <= index < 4]
    gate, up, send, signs = pl.pallas_call(
        functools.partial(hidden_kernel, group, parts, gathered, early),
        out_shape=(
            pltpu.VMEM((count, units), jnp.float32),
            pltpu.VMEM((count, units), jnp.float32),
            pltpu.VMEM((parts - 1, 2, count, units), jnp.bfloat16),
            pltpu.VMEM((len(early), count, units), jnp.float32),
        ),
        in_specs=[VMEM, HBM, HBM, HBM] + [VMEM] * len(held),
        out_specs=(VMEM, VMEM, VMEM, VMEM),
        scratch_shapes=[
            pltpu.VMEM((SLOTS, CHUNK, units), jnp.bfloat16),
            pltpu.VMEM((share // group, units), jnp.float32),
            pltpu.VMEM((share // group, units), jnp.float32),
            pltpu.VMEM((parts * count, share), jnp.bfloat16),
            pltpu.VMEM((parts * count * tiles_here, LANES), jnp.float32),
            pltpu.VMEM((parts * count, units), jnp.float32),
            pltpu.VMEM((parts * count, units), jnp.float32),
            pltpu.SemaphoreType.DMA((SLOTS + 2,)),
        ],
        compiler_params=pltpu.CompilerParams(vmem_limit_bytes=24 * MIB),
        cost_estimate=cost(2 * share * units, 4 * count * width * units),
    )(pieces, in_hbm(gate_scales), in_hbm(up_codes), in_hbm(up_scales), *[in_vmem(part) for part in held])

    others = [by_part(send[step - 1], -step) for step in range(1, parts)]
    columns = SPANS[0] * SPAN
    part, small = pl.pallas_call(
        functools.partial(columns_small_kernel, 0, SPAN),
        out_shape=(pltpu.VMEM((units, columns), jnp.bfloat16), pltpu.VMEM(hadamard.shape, hadamard.dtype)),
        in_specs=[HBM, ANY, HBM],
        out_specs=(VMEM, VMEM),
        scratch_shapes=[pltpu.SemaphoreType.DMA((SPANS[0] + 1,))],
        compiler_params=pltpu.CompilerParams(vmem_limit_bytes=2 * MIB),
        cost_estimate=cost(2 * units * columns),
    )(in_hbm(down_codes), send, in_hbm(hadamard))
    held = [part]
    first = columns

    turned, send = pl.pallas_call(
        rotate_kernel,
        out_shape=(pltpu.VMEM((count, units), jnp.float32), jax.ShapeDtypeStruct((count, units), jnp.bfloat16)),
        in_specs=[VMEM] * (2 + parts),
        out_specs=(VMEM, VMEM),
        compiler_params=pltpu.CompilerParams(vmem_limit_bytes=8 * MIB),
        cost_estimate=cost(16 * count * units),
    )(in_vmem(gate), in_vmem(up), in_vmem(small), *others)

    for index, bit in enumerate(bits):
        other = swap(send, bit)
        if 1 <= index < 4:
            columns = SPANS[index] * SPAN
            part, sign = pl.pallas_call(
                functools.partial(columns_kernel, first, SPAN, bit),
                out_shape=(pltpu.VMEM((units, columns), jnp.bfloat16), pltpu.VMEM((count, units), jnp.float32)),
                in_specs=[HBM, ANY],
                out_specs=(VMEM, VMEM),
                scratch_shapes=[pltpu.SemaphoreType.DMA((SPANS[index],))],
                compiler_params=pltpu.CompilerParams(vmem_limit_bytes=2 * MIB),
                cost_estimate=cost(2 * units * columns),
            )(in_hbm(down_codes), send)
            held.append(part)
            first += columns
        else:
            sign = signs[early.index(bit)]
        turned = turned * sign + other.astype(jnp.float32)
        send = turned.astype(jnp.bfloat16)

    order = [1] + [bit for bit in bits[1:]]
    spread = [0]
    for bit in reversed(order):
        spread = spread + [mask | bit for mask in spread]
    ahead = max(min((width - first) // SPAN, AHEAD), 1)
    keep, send = pl.pallas_call(
        functools.partial(down_kernel, 1.0 / math.sqrt(total_units), spread, len(held)),
        out_shape=(
            jax.ShapeDtypeStruct((devices // 2, own, tiles, LANES), jnp.float32),
            jax.ShapeDtypeStruct((devices // 2, own, tiles, LANES), jnp.bfloat16),
        ),
        in_specs=[VMEM, HBM] + [VMEM] * len(held),
        out_specs=(VMEM, VMEM),
        scratch_shapes=[
            pltpu.VMEM((count * tiles, LANES), jnp.float32),
            pltpu.VMEM((ahead, units, SPAN), jnp.bfloat16),
            pltpu.SemaphoreType.DMA((ahead,)),
        ],
        compiler_params=pltpu.CompilerParams(vmem_limit_bytes=20 * MIB),
        cost_estimate=cost(width * units, 2 * count * width * units),
    )(turned, in_hbm(down_codes), *[in_vmem(part) for part in held])
    summed = keep + swap(send, order[0]).astype(jnp.float32)
    for bit in order[1:]:
        half = summed.shape[0] // 2
        summed = summed[:half] + swap(summed[half:].astype(jnp.bfloat16), bit).astype(jnp.float32)
    return (summed.reshape(own, width) * down_scales[None, :]).astype(jnp.bfloat16)


def solution(mesh):
    in_specs = (
        P(("groups", "hx"), None),
        P(None, "hx"),
        P(None, "hx"),
        P(None, "hx"),
        P(None, "hx"),
        P("hx", None),
        P(),
        P(),
    )
    out_specs = P(("groups", "hx"), None)
    body = functools.partial(per_device, mesh.shape["groups"], mesh.shape["hx"])
    return jax.shard_map(body, mesh=mesh, in_specs=in_specs, out_specs=out_specs, check_vma=False)
```

```python
import functools
import math

import jax
import jax.numpy as jnp
from jax import lax
from jax.experimental import pallas as pl
from jax.experimental.pallas import tpu as pltpu
from jax.sharding import PartitionSpec as P

MIB = 2**20
F8 = jnp.float8_e4m3fn
LANES = 128
CHUNK = 512
SLOTS = 5
UNROLL = 2
ROWS = (2, 2, 2, 2)
SPAN = 512
AHEAD = 8
SPANS = (5, 3, 3, 4)

VMEM = pl.BlockSpec(memory_space=pltpu.VMEM)
HBM = pl.BlockSpec(memory_space=pltpu.HBM)
ANY = pl.BlockSpec(memory_space=pl.ANY)


def in_vmem(value):
    return pltpu.with_memory_space_constraint(value, pltpu.VMEM)


def in_hbm(value):
    return pltpu.with_memory_space_constraint(value, pltpu.HBM)


def fetch(source, target, sem):
    copy = pltpu.make_async_copy(source, target, sem)
    copy.start()
    return copy


def fetch_columns(first, step, codes_ref, out_ref, sems):
    copies = []
    for index in range(out_ref.shape[1] // step):
        here = codes_ref.at[:, pl.ds(first + index * step, step)]
        copies.append(fetch(here, out_ref.at[:, pl.ds(index * step, step)], sems.at[index]))
    return copies


def rows_columns_kernel(before, step, span, codes_ref, after_ref, down_ref, out_ref, same_ref, columns_ref, sems, column_sems):
    copies = fetch_columns(0, span, down_ref, columns_ref, column_sems)
    rows_kernel(before, step, codes_ref, after_ref, out_ref, same_ref, sems)
    for copy in copies:
        copy.wait()


def columns_kernel(first, step, bit, codes_ref, after_ref, out_ref, sign_ref, sems):
    copies = fetch_columns(first, step, codes_ref, out_ref, sems)
    sign = 1.0 - 2.0 * ((lax.axis_index("hx") // bit) % 2).astype(jnp.float32)
    sign_ref[...] = jnp.full(sign_ref.shape, sign, jnp.float32)
    for copy in copies:
        copy.wait()


def rows_kernel(before, step, codes_ref, after_ref, out_ref, same_ref, sems):
    copies = [fetch(after_ref, same_ref, sems.at[out_ref.shape[0] // step])]
    share = codes_ref.shape[0] // lax.axis_size("groups")
    first = pl.multiple_of(lax.axis_index("groups") * share + before, step)
    for index in range(out_ref.shape[0] // step):
        here = codes_ref.at[pl.ds(first + index * step, step), :]
        copies.append(fetch(here, out_ref.at[pl.ds(index * step, step), :], sems.at[index]))
    for copy in copies:
        copy.wait()


def columns_small_kernel(first, step, codes_ref, after_ref, hadamard_ref, out_ref, small_ref, sems):
    copies = [fetch(hadamard_ref, small_ref, sems.at[out_ref.shape[1] // step])]
    copies += fetch_columns(first, step, codes_ref, out_ref, sems)
    for copy in copies:
        copy.wait()


def tiles_kernel(mine_ref, *refs):
    others, out_ref, wide_ref = refs[:-2], refs[-2], refs[-1]
    _, own, tiles, lanes = out_ref.shape
    first = pl.multiple_of(lax.axis_index("groups") * (tiles * lanes), tiles * lanes)
    for index, token_ref in enumerate((mine_ref,) + others):
        for at in range(own):
            row = token_ref[at : at + 1, pl.ds(first, tiles * lanes)].astype(jnp.float32)
            for tile in range(tiles):
                wide_ref[tile : tile + 1, :] = row[:, tile * lanes : (tile + 1) * lanes]
            out_ref[index, at] = wide_ref[...].astype(out_ref.dtype)


def rotate(gate, up, hadamard):
    count, units = gate.shape
    small = hadamard.shape[0]
    high = units // small
    hidden = gate / (1.0 + jnp.exp(-gate)) * up
    tall = jnp.concatenate([hidden[:, at * small : (at + 1) * small] for at in range(high)], axis=0)
    coarse = tall.astype(jnp.bfloat16)
    fine = (tall - coarse.astype(jnp.float32)).astype(jnp.bfloat16)
    factor = hadamard.astype(jnp.bfloat16)
    tall = jnp.dot(coarse, factor, preferred_element_type=jnp.float32) + jnp.dot(
        fine, factor, preferred_element_type=jnp.float32
    )
    blocks = [tall[at * count : (at + 1) * count] for at in range(high)]
    bit = 1
    while bit < high:
        for at in range(high):
            if at & bit == 0:
                blocks[at], blocks[at | bit] = blocks[at] + blocks[at | bit], blocks[at] - blocks[at | bit]
        bit *= 2
    return jnp.concatenate(blocks, axis=1)


def rotate_kernel(gate_ref, up_ref, hadamard_ref, *refs):
    others, out_ref, send_ref = refs[:-2], refs[-2], refs[-1]
    gate = gate_ref[...]
    up = up_ref[...]
    for other in others:
        gate = gate + other[0].astype(jnp.float32)
        up = up + other[1].astype(jnp.float32)
    turned = rotate(gate, up, hadamard_ref[...])
    out_ref[...] = turned
    send_ref[...] = turned.astype(send_ref.dtype)


def hidden_kernel(group, parts, masks, bits, *refs):
    pieces_ref, gate_scales_ref, up_codes_ref, up_scales_ref = refs[:4]
    held = refs[4:-12]
    gate_ref, up_ref, send_ref, signs_ref, buffers, gate_rows, up_rows, tokens_ref, wide_ref, gate_sum, up_sum, sems = refs[-12:]
    depth, rows, units = buffers.shape
    slots, own, tiles, lanes = pieces_ref.shape
    count = slots // parts * own
    share = tiles * lanes
    steps = share // rows
    mine = lax.axis_index("groups")

    def copy(step):
        slot = lax.rem(step, depth)
        first = pl.multiple_of(mine * share + step * rows, rows)
        return pltpu.make_async_copy(up_codes_ref.at[pl.ds(first, rows), :], buffers.at[slot], sems.at[slot])

    first = pl.multiple_of(mine * (share // group), share // group)
    small_copies = [
        fetch(gate_scales_ref.at[pl.ds(first, share // group), :], gate_rows, sems.at[depth]),
        fetch(up_scales_ref.at[pl.ds(first, share // group), :], up_rows, sems.at[depth + 1]),
    ]
    for step in range(min(depth, steps)):
        copy(step).start()
    me = lax.axis_index("hx")
    for index, bit in enumerate(bits):
        sign = 1.0 - 2.0 * ((me // bit) % 2).astype(jnp.float32)
        signs_ref[index] = jnp.full((count, units), sign, jnp.float32)
    for slot, mask in enumerate(masks):
        for part in range(parts):
            for at in range(own):
                where = pl.multiple_of((part * count + (me ^ mask) * own + at) * tiles, tiles)
                wide_ref[pl.ds(where, tiles), :] = pieces_ref[slot * parts + part, at].astype(jnp.float32)
    for tile in range(tiles):
        here = wide_ref[pl.ds(tile, parts * count, stride=tiles), :]
        tokens_ref[:, tile * lanes : (tile + 1) * lanes] = here.astype(jnp.bfloat16)
    gate_sum[...] = jnp.zeros_like(gate_sum)
    up_sum[...] = jnp.zeros_like(up_sum)
    low_half = lax.broadcasted_iota(jnp.int32, (parts * count, 2 * group), 1) < group
    for small_copy in small_copies:
        small_copy.wait()

    def add(total_ref, scales_ref, step, codes):
        for pair in range(rows // (2 * group)):
            index = step * (rows // (2 * group)) + pair
            two = tokens_ref[:, pl.ds(pl.multiple_of(index * 2 * group, 2 * group), 2 * group)]
            none = jnp.zeros_like(two)
            stacked = jnp.concatenate([jnp.where(low_half, two, none), jnp.where(low_half, none, two)], axis=0)
            sums = jnp.dot(stacked, codes(pair * 2 * group).astype(F8), preferred_element_type=jnp.float32)
            total_ref[...] += (
                sums[: parts * count] * scales_ref[pl.ds(2 * index, 1), :]
                + sums[parts * count :] * scales_ref[pl.ds(2 * index + 1, 1), :]
            )

    before = 0
    for part in held:

        def body(step, carry, part=part, before=before):
            slot = lax.rem(step, depth)

            def in_part(first):
                return part[pl.ds(pl.multiple_of((step - before) * rows + first, 2 * group), 2 * group), :]

            def in_buffer(first):
                return buffers[slot, first : first + 2 * group, :]

            add(gate_sum, gate_rows, step, in_part)
            copy(step).wait()
            add(up_sum, up_rows, step, in_buffer)

            @pl.when(step + depth < steps)
            def _():
                copy(step + depth).start()

            return carry

        lax.fori_loop(before, before + part.shape[0] // rows, body, 0, unroll=UNROLL)
        before += part.shape[0] // rows
    gate_ref[...] = gate_sum[:count, :]
    up_ref[...] = up_sum[:count, :]
    for part in range(1, parts):
        span = slice(part * count, (part + 1) * count)
        send_ref[part - 1, 0] = gate_sum[span, :].astype(send_ref.dtype)
        send_ref[part - 1, 1] = up_sum[span, :].astype(send_ref.dtype)


def down_kernel(scale, masks, parts, *refs):
    turned_ref, codes_ref = refs[:2]
    held = refs[2 : 2 + parts]
    keep_ref, send_ref, wide_ref, buffers, sems = refs[2 + parts :]
    depth, _, span = buffers.shape
    begin = sum(part.shape[1] for part in held)
    total = (codes_ref.shape[1] - begin) // span

    def copy(step):
        here = codes_ref.at[:, pl.ds(begin + step * span, span)]
        return pltpu.make_async_copy(here, buffers.at[step % depth], sems.at[step % depth])

    for step in range(min(depth, total)):
        copy(step).start()
    me = lax.axis_index("hx")
    half, own, tiles, lanes = keep_ref.shape
    count = turned_ref.shape[0]
    rotated = (turned_ref[...] * scale).astype(jnp.bfloat16)
    row = lax.broadcasted_iota(jnp.int32, (count, count), 0)
    col = lax.broadcasted_iota(jnp.int32, (count, count), 1)
    slot = row // own
    mask = jnp.zeros_like(slot)
    for index in range(len(masks).bit_length() - 1):
        mask = mask | jnp.where((jnp.right_shift(slot, index) & 1) == 1, masks[1 << index], 0)
    order = ((slot * 0 + me) ^ mask) * own + (row - slot * own) == col
    rotated = jnp.dot(order.astype(jnp.bfloat16), rotated, preferred_element_type=jnp.float32).astype(jnp.bfloat16)

    def put(first, codes):
        sums = jnp.dot(rotated, codes.astype(F8), preferred_element_type=jnp.float32)
        for tile in range(span // lanes):
            wide_ref[pl.ds(first // lanes + tile, count, stride=tiles), :] = sums[:, tile * lanes : (tile + 1) * lanes]

    def put_streamed(step):
        copy(step).wait()
        put(begin + step * span, buffers[step % depth])
        if step + depth < total:
            copy(step + depth).start()

    base = 0
    for part in held:
        for first in range(0, part.shape[1], span):
            put(base + first, part[:, first : first + span])
        base += part.shape[1]
    for step in range(total):
        put_streamed(step)
    for index in range(half):
        for at in range(own):
            first = (index * own + at) * tiles
            keep_ref[index, at] = wide_ref[first : first + tiles, :]
            first += half * own * tiles
            send_ref[index, at] = wide_ref[first : first + tiles, :].astype(send_ref.dtype)


def per_device(
    parts, devices, tokens, gate_codes, gate_scales, up_codes, up_scales, down_codes, down_scales, hadamard
):
    width, units = gate_codes.shape
    group = width // gate_scales.shape[0]
    own = tokens.shape[0]
    count = own * devices
    total_units = units * devices
    bits = [1 << level for level in range(devices.bit_length() - 1)]
    tiles = width // LANES

    def swap(value, bit):
        return lax.ppermute(value, "hx", [(at, at ^ bit) for at in range(devices)])

    def cost(nbytes, flops=0):
        return pl.CostEstimate(flops=flops, bytes_accessed=nbytes, transcendentals=0)

    share = width // parts
    tiles_here = tiles // parts

    def by_part(value, step):
        return lax.ppermute(value, "groups", [(at, (at + step) % parts) for at in range(parts)])

    def some_rows(index, first, after, in_space):
        rows = ROWS[index] * CHUNK
        return pl.pallas_call(
            functools.partial(rows_kernel, first, CHUNK),
            out_shape=(pltpu.VMEM((rows, units), jnp.bfloat16), pltpu.VMEM(after.shape, after.dtype)),
            in_specs=[HBM, in_space],
            out_specs=(VMEM, VMEM),
            scratch_shapes=[pltpu.SemaphoreType.DMA((ROWS[index] + 1,))],
            compiler_params=pltpu.CompilerParams(vmem_limit_bytes=2 * MIB),
            cost_estimate=cost(2 * rows * units),
        )(in_hbm(gate_codes), after)

    others = [by_part(tokens, step) for step in range(1, parts)]
    part, mine = some_rows(0, 0, in_hbm(tokens), HBM)
    held = [part]
    first = part.shape[0]
    pieces = pl.pallas_call(
        tiles_kernel,
        out_shape=jax.ShapeDtypeStruct((parts, own, tiles_here, LANES), tokens.dtype),
        in_specs=[VMEM] * parts,
        out_specs=VMEM,
        scratch_shapes=[pltpu.VMEM((tiles_here, LANES), jnp.float32)],
        compiler_params=pltpu.CompilerParams(vmem_limit_bytes=2 * MIB),
        cost_estimate=cost(4 * own * width),
    )(in_vmem(mine), *others)
    gathered = [0]
    for index, bit in enumerate(reversed(bits)):
        other = swap(pieces, bit)
        if index + 1 < len(ROWS):
            if index + 2 < len(ROWS):
                part, pieces = some_rows(index + 1, first, pieces, ANY)
            else:
                part, pieces, down_part = pl.pallas_call(
                    functools.partial(rows_columns_kernel, first, CHUNK, SPAN),
                    out_shape=(
                        pltpu.VMEM((ROWS[-1] * CHUNK, units), jnp.bfloat16),
                        pltpu.VMEM(pieces.shape, pieces.dtype),
                        pltpu.VMEM((units, SPAN), jnp.bfloat16),
                    ),
                    in_specs=[HBM, ANY, HBM],
                    out_specs=(VMEM, VMEM, VMEM),
                    scratch_shapes=[pltpu.SemaphoreType.DMA((ROWS[-1] + 1,)), pltpu.SemaphoreType.DMA((1,))],
                    compiler_params=pltpu.CompilerParams(vmem_limit_bytes=2 * MIB),
                    cost_estimate=cost(2 * ROWS[-1] * CHUNK * units + 2 * SPAN * units),
                )(in_hbm(gate_codes), pieces, in_hbm(down_codes))
            held.append(part)
            first += part.shape[0]
        pieces = jnp.concatenate([pieces, other], axis=0)
        gathered = gathered + [mask | bit for mask in gathered]

    early = [bit for index, bit in enumerate(bits) if not 1 <= index < 4]
    gate, up, send, signs = pl.pallas_call(
        functools.partial(hidden_kernel, group, parts, gathered, early),
        out_shape=(
            pltpu.VMEM((count, units), jnp.float32),
            pltpu.VMEM((count, units), jnp.float32),
            pltpu.VMEM((parts - 1, 2, count, units), jnp.bfloat16),
            pltpu.VMEM((len(early), count, units), jnp.float32),
        ),
        in_specs=[VMEM, HBM, HBM, HBM] + [VMEM] * len(held),
        out_specs=(VMEM, VMEM, VMEM, VMEM),
        scratch_shapes=[
            pltpu.VMEM((SLOTS, CHUNK, units), jnp.bfloat16),
            pltpu.VMEM((share // group, units), jnp.float32),
            pltpu.VMEM((share // group, units), jnp.float32),
            pltpu.VMEM((parts * count, share), jnp.bfloat16),
            pltpu.VMEM((parts * count * tiles_here, LANES), jnp.float32),
            pltpu.VMEM((parts * count, units), jnp.float32),
            pltpu.VMEM((parts * count, units), jnp.float32),
            pltpu.SemaphoreType.DMA((SLOTS + 2,)),
        ],
        compiler_params=pltpu.CompilerParams(vmem_limit_bytes=24 * MIB),
        cost_estimate=cost(2 * share * units, 4 * count * width * units),
    )(pieces, in_hbm(gate_scales), in_hbm(up_codes), in_hbm(up_scales), *[in_vmem(part) for part in held])

    others = [by_part(send[step - 1], -step) for step in range(1, parts)]
    columns = SPANS[0] * SPAN
    part, small = pl.pallas_call(
        functools.partial(columns_small_kernel, SPAN, SPAN),
        out_shape=(pltpu.VMEM((units, columns), jnp.bfloat16), pltpu.VMEM(hadamard.shape, hadamard.dtype)),
        in_specs=[HBM, ANY, HBM],
        out_specs=(VMEM, VMEM),
        scratch_shapes=[pltpu.SemaphoreType.DMA((SPANS[0] + 1,))],
        compiler_params=pltpu.CompilerParams(vmem_limit_bytes=2 * MIB),
        cost_estimate=cost(2 * units * columns),
    )(in_hbm(down_codes), send, in_hbm(hadamard))
    held = [down_part, part]
    first = SPAN + columns

    turned, send = pl.pallas_call(
        rotate_kernel,
        out_shape=(pltpu.VMEM((count, units), jnp.float32), jax.ShapeDtypeStruct((count, units), jnp.bfloat16)),
        in_specs=[VMEM] * (2 + parts),
        out_specs=(VMEM, VMEM),
        compiler_params=pltpu.CompilerParams(vmem_limit_bytes=8 * MIB),
        cost_estimate=cost(16 * count * units),
    )(in_vmem(gate), in_vmem(up), in_vmem(small), *others)

    for index, bit in enumerate(bits):
        other = swap(send, bit)
        if 1 <= index < 4:
            columns = SPANS[index] * SPAN
            part, sign = pl.pallas_call(
                functools.partial(columns_kernel, first, SPAN, bit),
                out_shape=(pltpu.VMEM((units, columns), jnp.bfloat16), pltpu.VMEM((count, units), jnp.float32)),
                in_specs=[HBM, ANY],
                out_specs=(VMEM, VMEM),
                scratch_shapes=[pltpu.SemaphoreType.DMA((SPANS[index],))],
                compiler_params=pltpu.CompilerParams(vmem_limit_bytes=2 * MIB),
                cost_estimate=cost(2 * units * columns),
            )(in_hbm(down_codes), send)
            held.append(part)
            first += columns
        else:
            sign = signs[early.index(bit)]
        turned = turned * sign + other.astype(jnp.float32)
        send = turned.astype(jnp.bfloat16)

    order = [1] + [bit for bit in bits[1:]]
    spread = [0]
    for bit in reversed(order):
        spread = spread + [mask | bit for mask in spread]
    ahead = max(min((width - first) // SPAN, AHEAD), 1)
    keep, send = pl.pallas_call(
        functools.partial(down_kernel, 1.0 / math.sqrt(total_units), spread, len(held)),
        out_shape=(
            jax.ShapeDtypeStruct((devices // 2, own, tiles, LANES), jnp.float32),
            jax.ShapeDtypeStruct((devices // 2, own, tiles, LANES), jnp.bfloat16),
        ),
        in_specs=[VMEM, HBM] + [VMEM] * len(held),
        out_specs=(VMEM, VMEM),
        scratch_shapes=[
            pltpu.VMEM((count * tiles, LANES), jnp.float32),
            pltpu.VMEM((ahead, units, SPAN), jnp.bfloat16),
            pltpu.SemaphoreType.DMA((ahead,)),
        ],
        compiler_params=pltpu.CompilerParams(vmem_limit_bytes=20 * MIB),
        cost_estimate=cost(width * units, 2 * count * width * units),
    )(turned, in_hbm(down_codes), *[in_vmem(part) for part in held])
    summed = keep + swap(send, order[0]).astype(jnp.float32)
    for bit in order[1:]:
        half = summed.shape[0] // 2
        summed = summed[:half] + swap(summed[half:].astype(jnp.bfloat16), bit).astype(jnp.float32)
    return (summed.reshape(own, width) * down_scales[None, :]).astype(jnp.bfloat16)


def solution(mesh):
    in_specs = (
        P(("groups", "hx"), None),
        P(None, "hx"),
        P(None, "hx"),
        P(None, "hx"),
        P(None, "hx"),
        P("hx", None),
        P(),
        P(),
    )
    out_specs = P(("groups", "hx"), None)
    body = functools.partial(per_device, mesh.shape["groups"], mesh.shape["hx"])
    return jax.shard_map(body, mesh=mesh, in_specs=in_specs, out_specs=out_specs, check_vma=False)
```

```python
import functools
import math

import jax
import jax.numpy as jnp
from jax import lax
from jax.experimental import pallas as pl
from jax.experimental.pallas import tpu as pltpu
from jax.sharding import PartitionSpec as P

MIB = 2**20
F8 = jnp.float8_e4m3fn
LANES = 128
CHUNK = 512
SLOTS = 5
UNROLL = 2
ROWS = (2, 2, 2, 2)
SPAN = 512
AHEAD = 8
SPANS = (5, 3, 3, 3)

VMEM = pl.BlockSpec(memory_space=pltpu.VMEM)
HBM = pl.BlockSpec(memory_space=pltpu.HBM)
ANY = pl.BlockSpec(memory_space=pl.ANY)


def in_vmem(value):
    return pltpu.with_memory_space_constraint(value, pltpu.VMEM)


def in_hbm(value):
    return pltpu.with_memory_space_constraint(value, pltpu.HBM)


def fetch(source, target, sem):
    copy = pltpu.make_async_copy(source, target, sem)
    copy.start()
    return copy


def fetch_columns(first, step, codes_ref, out_ref, sems):
    copies = []
    for index in range(out_ref.shape[1] // step):
        here = codes_ref.at[:, pl.ds(first + index * step, step)]
        copies.append(fetch(here, out_ref.at[:, pl.ds(index * step, step)], sems.at[index]))
    return copies


def rows_columns_kernel(before, step, span, codes_ref, after_ref, down_ref, out_ref, same_ref, columns_ref, sems, column_sems):
    copies = fetch_columns(0, span, down_ref, columns_ref, column_sems)
    rows_kernel(before, step, codes_ref, after_ref, out_ref, same_ref, sems)
    for copy in copies:
        copy.wait()


def columns_kernel(first, step, bit, codes_ref, after_ref, out_ref, sign_ref, sems):
    copies = fetch_columns(first, step, codes_ref, out_ref, sems)
    sign = 1.0 - 2.0 * ((lax.axis_index("hx") // bit) % 2).astype(jnp.float32)
    sign_ref[...] = jnp.full(sign_ref.shape, sign, jnp.float32)
    for copy in copies:
        copy.wait()


def rows_kernel(before, step, codes_ref, after_ref, out_ref, same_ref, sems):
    copies = [fetch(after_ref, same_ref, sems.at[out_ref.shape[0] // step])]
    share = codes_ref.shape[0] // lax.axis_size("groups")
    first = pl.multiple_of(lax.axis_index("groups") * share + before, step)
    for index in range(out_ref.shape[0] // step):
        here = codes_ref.at[pl.ds(first + index * step, step), :]
        copies.append(fetch(here, out_ref.at[pl.ds(index * step, step), :], sems.at[index]))
    for copy in copies:
        copy.wait()


def columns_small_kernel(first, step, codes_ref, after_ref, hadamard_ref, out_ref, small_ref, sems):
    copies = [fetch(hadamard_ref, small_ref, sems.at[out_ref.shape[1] // step])]
    copies += fetch_columns(first, step, codes_ref, out_ref, sems)
    for copy in copies:
        copy.wait()


def tiles_kernel(mine_ref, *refs):
    others, out_ref, wide_ref = refs[:-2], refs[-2], refs[-1]
    _, own, tiles, lanes = out_ref.shape
    first = pl.multiple_of(lax.axis_index("groups") * (tiles * lanes), tiles * lanes)
    for index, token_ref in enumerate((mine_ref,) + others):
        for at in range(own):
            row = token_ref[at : at + 1, pl.ds(first, tiles * lanes)].astype(jnp.float32)
            for tile in range(tiles):
                wide_ref[tile : tile + 1, :] = row[:, tile * lanes : (tile + 1) * lanes]
            out_ref[index, at] = wide_ref[...].astype(out_ref.dtype)


def rotate(gate, up, hadamard):
    count, units = gate.shape
    small = hadamard.shape[0]
    high = units // small
    hidden = gate / (1.0 + jnp.exp(-gate)) * up
    tall = jnp.concatenate([hidden[:, at * small : (at + 1) * small] for at in range(high)], axis=0)
    coarse = tall.astype(jnp.bfloat16)
    fine = (tall - coarse.astype(jnp.float32)).astype(jnp.bfloat16)
    factor = hadamard.astype(jnp.bfloat16)
    tall = jnp.dot(coarse, factor, preferred_element_type=jnp.float32) + jnp.dot(
        fine, factor, preferred_element_type=jnp.float32
    )
    blocks = [tall[at * count : (at + 1) * count] for at in range(high)]
    bit = 1
    while bit < high:
        for at in range(high):
            if at & bit == 0:
                blocks[at], blocks[at | bit] = blocks[at] + blocks[at | bit], blocks[at] - blocks[at | bit]
        bit *= 2
    return jnp.concatenate(blocks, axis=1)


def rotate_kernel(gate_ref, up_ref, hadamard_ref, *refs):
    others, out_ref, send_ref = refs[:-2], refs[-2], refs[-1]
    gate = gate_ref[...]
    up = up_ref[...]
    for other in others:
        gate = gate + other[0].astype(jnp.float32)
        up = up + other[1].astype(jnp.float32)
    turned = rotate(gate, up, hadamard_ref[...])
    out_ref[...] = turned
    send_ref[...] = turned.astype(send_ref.dtype)


def hidden_kernel(group, parts, masks, bits, *refs):
    pieces_ref, gate_scales_ref, up_codes_ref, up_scales_ref = refs[:4]
    held = refs[4:-12]
    gate_ref, up_ref, send_ref, signs_ref, buffers, gate_rows, up_rows, tokens_ref, wide_ref, gate_sum, up_sum, sems = refs[-12:]
    depth, rows, units = buffers.shape
    slots, own, tiles, lanes = pieces_ref.shape
    count = slots // parts * own
    share = tiles * lanes
    steps = share // rows
    mine = lax.axis_index("groups")

    def copy(step):
        slot = lax.rem(step, depth)
        first = pl.multiple_of(mine * share + step * rows, rows)
        return pltpu.make_async_copy(up_codes_ref.at[pl.ds(first, rows), :], buffers.at[slot], sems.at[slot])

    first = pl.multiple_of(mine * (share // group), share // group)
    small_copies = [
        fetch(gate_scales_ref.at[pl.ds(first, share // group), :], gate_rows, sems.at[depth]),
        fetch(up_scales_ref.at[pl.ds(first, share // group), :], up_rows, sems.at[depth + 1]),
    ]
    for step in range(min(depth, steps)):
        copy(step).start()
    me = lax.axis_index("hx")
    for index, bit in enumerate(bits):
        sign = 1.0 - 2.0 * ((me // bit) % 2).astype(jnp.float32)
        signs_ref[index] = jnp.full((count, units), sign, jnp.float32)
    for slot, mask in enumerate(masks):
        for part in range(parts):
            for at in range(own):
                where = pl.multiple_of((part * count + (me ^ mask) * own + at) * tiles, tiles)
                wide_ref[pl.ds(where, tiles), :] = pieces_ref[slot * parts + part, at].astype(jnp.float32)
    for tile in range(tiles):
        here = wide_ref[pl.ds(tile, parts * count, stride=tiles), :]
        tokens_ref[:, tile * lanes : (tile + 1) * lanes] = here.astype(jnp.bfloat16)
    gate_sum[...] = jnp.zeros_like(gate_sum)
    up_sum[...] = jnp.zeros_like(up_sum)
    low_half = lax.broadcasted_iota(jnp.int32, (parts * count, 2 * group), 1) < group
    for small_copy in small_copies:
        small_copy.wait()

    def add(total_ref, scales_ref, step, codes):
        for pair in range(rows // (2 * group)):
            index = step * (rows // (2 * group)) + pair
            two = tokens_ref[:, pl.ds(pl.multiple_of(index * 2 * group, 2 * group), 2 * group)]
            none = jnp.zeros_like(two)
            stacked = jnp.concatenate([jnp.where(low_half, two, none), jnp.where(low_half, none, two)], axis=0)
            sums = jnp.dot(stacked, codes(pair * 2 * group).astype(F8), preferred_element_type=jnp.float32)
            total_ref[...] += (
                sums[: parts * count] * scales_ref[pl.ds(2 * index, 1), :]
                + sums[parts * count :] * scales_ref[pl.ds(2 * index + 1, 1), :]
            )

    before = 0
    for part in held:

        def body(step, carry, part=part, before=before):
            slot = lax.rem(step, depth)

            def in_part(first):
                return part[pl.ds(pl.multiple_of((step - before) * rows + first, 2 * group), 2 * group), :]

            def in_buffer(first):
                return buffers[slot, first : first + 2 * group, :]

            add(gate_sum, gate_rows, step, in_part)
            copy(step).wait()
            add(up_sum, up_rows, step, in_buffer)

            @pl.when(step + depth < steps)
            def _():
                copy(step + depth).start()

            return carry

        lax.fori_loop(before, before + part.shape[0] // rows, body, 0, unroll=UNROLL)
        before += part.shape[0] // rows
    gate_ref[...] = gate_sum[:count, :]
    up_ref[...] = up_sum[:count, :]
    for part in range(1, parts):
        span = slice(part * count, (part + 1) * count)
        send_ref[part - 1, 0] = gate_sum[span, :].astype(send_ref.dtype)
        send_ref[part - 1, 1] = up_sum[span, :].astype(send_ref.dtype)


def down_kernel(scale, masks, parts, *refs):
    turned_ref, codes_ref = refs[:2]
    held = refs[2 : 2 + parts]
    keep_ref, send_ref, wide_ref, buffers, sems = refs[2 + parts :]
    depth, _, span = buffers.shape
    begin = sum(part.shape[1] for part in held)
    total = (codes_ref.shape[1] - begin) // span

    def copy(step):
        here = codes_ref.at[:, pl.ds(begin + step * span, span)]
        return pltpu.make_async_copy(here, buffers.at[step % depth], sems.at[step % depth])

    for step in range(min(depth, total)):
        copy(step).start()
    me = lax.axis_index("hx")
    half, own, tiles, lanes = keep_ref.shape
    count = turned_ref.shape[0]
    rotated = (turned_ref[...] * scale).astype(jnp.bfloat16)
    row = lax.broadcasted_iota(jnp.int32, (count, count), 0)
    col = lax.broadcasted_iota(jnp.int32, (count, count), 1)
    slot = row // own
    mask = jnp.zeros_like(slot)
    for index in range(len(masks).bit_length() - 1):
        mask = mask | jnp.where((jnp.right_shift(slot, index) & 1) == 1, masks[1 << index], 0)
    order = ((slot * 0 + me) ^ mask) * own + (row - slot * own) == col
    rotated = jnp.dot(order.astype(jnp.bfloat16), rotated, preferred_element_type=jnp.float32).astype(jnp.bfloat16)

    def put(first, codes):
        sums = jnp.dot(rotated, codes.astype(F8), preferred_element_type=jnp.float32)
        for tile in range(span // lanes):
            wide_ref[pl.ds(first // lanes + tile, count, stride=tiles), :] = sums[:, tile * lanes : (tile + 1) * lanes]

    def put_streamed(step):
        copy(step).wait()
        put(begin + step * span, buffers[step % depth])
        if step + depth < total:
            copy(step + depth).start()

    base = 0
    for part in held:
        for first in range(0, part.shape[1], span):
            put(base + first, part[:, first : first + span])
        base += part.shape[1]
    for step in range(total):
        put_streamed(step)
    for index in range(half):
        for at in range(own):
            first = (index * own + at) * tiles
            keep_ref[index, at] = wide_ref[first : first + tiles, :]
            first += half * own * tiles
            send_ref[index, at] = wide_ref[first : first + tiles, :].astype(send_ref.dtype)


def per_device(
    parts, devices, tokens, gate_codes, gate_scales, up_codes, up_scales, down_codes, down_scales, hadamard
):
    width, units = gate_codes.shape
    group = width // gate_scales.shape[0]
    own = tokens.shape[0]
    count = own * devices
    total_units = units * devices
    bits = [1 << level for level in range(devices.bit_length() - 1)]
    tiles = width // LANES

    def swap(value, bit):
        return lax.ppermute(value, "hx", [(at, at ^ bit) for at in range(devices)])

    def cost(nbytes, flops=0):
        return pl.CostEstimate(flops=flops, bytes_accessed=nbytes, transcendentals=0)

    share = width // parts
    tiles_here = tiles // parts

    def by_part(value, step):
        return lax.ppermute(value, "groups", [(at, (at + step) % parts) for at in range(parts)])

    def some_rows(index, first, after, in_space):
        rows = ROWS[index] * CHUNK
        return pl.pallas_call(
            functools.partial(rows_kernel, first, CHUNK),
            out_shape=(pltpu.VMEM((rows, units), jnp.bfloat16), pltpu.VMEM(after.shape, after.dtype)),
            in_specs=[HBM, in_space],
            out_specs=(VMEM, VMEM),
            scratch_shapes=[pltpu.SemaphoreType.DMA((ROWS[index] + 1,))],
            compiler_params=pltpu.CompilerParams(vmem_limit_bytes=2 * MIB),
            cost_estimate=cost(2 * rows * units),
        )(in_hbm(gate_codes), after)

    others = [by_part(tokens, step) for step in range(1, parts)]
    part, mine = some_rows(0, 0, in_hbm(tokens), HBM)
    held = [part]
    first = part.shape[0]
    pieces = pl.pallas_call(
        tiles_kernel,
        out_shape=jax.ShapeDtypeStruct((parts, own, tiles_here, LANES), tokens.dtype),
        in_specs=[VMEM] * parts,
        out_specs=VMEM,
        scratch_shapes=[pltpu.VMEM((tiles_here, LANES), jnp.float32)],
        compiler_params=pltpu.CompilerParams(vmem_limit_bytes=2 * MIB),
        cost_estimate=cost(4 * own * width),
    )(in_vmem(mine), *others)
    gathered = [0]
    for index, bit in enumerate(reversed(bits)):
        other = swap(pieces, bit)
        if index + 1 < len(ROWS):
            if index + 2 < len(ROWS):
                part, pieces = some_rows(index + 1, first, pieces, ANY)
            else:
                part, pieces, down_part = pl.pallas_call(
                    functools.partial(rows_columns_kernel, first, CHUNK, SPAN),
                    out_shape=(
                        pltpu.VMEM((ROWS[-1] * CHUNK, units), jnp.bfloat16),
                        pltpu.VMEM(pieces.shape, pieces.dtype),
                        pltpu.VMEM((units, 2 * SPAN), jnp.bfloat16),
                    ),
                    in_specs=[HBM, ANY, HBM],
                    out_specs=(VMEM, VMEM, VMEM),
                    scratch_shapes=[pltpu.SemaphoreType.DMA((ROWS[-1] + 1,)), pltpu.SemaphoreType.DMA((2,))],
                    compiler_params=pltpu.CompilerParams(vmem_limit_bytes=2 * MIB),
                    cost_estimate=cost(2 * ROWS[-1] * CHUNK * units + 2 * SPAN * units),
                )(in_hbm(gate_codes), pieces, in_hbm(down_codes))
            held.append(part)
            first += part.shape[0]
        pieces = jnp.concatenate([pieces, other], axis=0)
        gathered = gathered + [mask | bit for mask in gathered]

    early = [bit for index, bit in enumerate(bits) if not 1 <= index < 4]
    gate, up, send, signs = pl.pallas_call(
        functools.partial(hidden_kernel, group, parts, gathered, early),
        out_shape=(
            pltpu.VMEM((count, units), jnp.float32),
            pltpu.VMEM((count, units), jnp.float32),
            pltpu.VMEM((parts - 1, 2, count, units), jnp.bfloat16),
            pltpu.VMEM((len(early), count, units), jnp.float32),
        ),
        in_specs=[VMEM, HBM, HBM, HBM] + [VMEM] * len(held),
        out_specs=(VMEM, VMEM, VMEM, VMEM),
        scratch_shapes=[
            pltpu.VMEM((SLOTS, CHUNK, units), jnp.bfloat16),
            pltpu.VMEM((share // group, units), jnp.float32),
            pltpu.VMEM((share // group, units), jnp.float32),
            pltpu.VMEM((parts * count, share), jnp.bfloat16),
            pltpu.VMEM((parts * count * tiles_here, LANES), jnp.float32),
            pltpu.VMEM((parts * count, units), jnp.float32),
            pltpu.VMEM((parts * count, units), jnp.float32),
            pltpu.SemaphoreType.DMA((SLOTS + 2,)),
        ],
        compiler_params=pltpu.CompilerParams(vmem_limit_bytes=24 * MIB),
        cost_estimate=cost(2 * share * units, 4 * count * width * units),
    )(pieces, in_hbm(gate_scales), in_hbm(up_codes), in_hbm(up_scales), *[in_vmem(part) for part in held])

    others = [by_part(send[step - 1], -step) for step in range(1, parts)]
    columns = SPANS[0] * SPAN
    part, small = pl.pallas_call(
        functools.partial(columns_small_kernel, 2 * SPAN, SPAN),
        out_shape=(pltpu.VMEM((units, columns), jnp.bfloat16), pltpu.VMEM(hadamard.shape, hadamard.dtype)),
        in_specs=[HBM, ANY, HBM],
        out_specs=(VMEM, VMEM),
        scratch_shapes=[pltpu.SemaphoreType.DMA((SPANS[0] + 1,))],
        compiler_params=pltpu.CompilerParams(vmem_limit_bytes=2 * MIB),
        cost_estimate=cost(2 * units * columns),
    )(in_hbm(down_codes), send, in_hbm(hadamard))
    held = [down_part, part]
    first = 2 * SPAN + columns

    turned, send = pl.pallas_call(
        rotate_kernel,
        out_shape=(pltpu.VMEM((count, units), jnp.float32), jax.ShapeDtypeStruct((count, units), jnp.bfloat16)),
        in_specs=[VMEM] * (2 + parts),
        out_specs=(VMEM, VMEM),
        compiler_params=pltpu.CompilerParams(vmem_limit_bytes=8 * MIB),
        cost_estimate=cost(16 * count * units),
    )(in_vmem(gate), in_vmem(up), in_vmem(small), *others)

    for index, bit in enumerate(bits):
        other = swap(send, bit)
        if 1 <= index < 4:
            columns = SPANS[index] * SPAN
            part, sign = pl.pallas_call(
                functools.partial(columns_kernel, first, SPAN, bit),
                out_shape=(pltpu.VMEM((units, columns), jnp.bfloat16), pltpu.VMEM((count, units), jnp.float32)),
                in_specs=[HBM, ANY],
                out_specs=(VMEM, VMEM),
                scratch_shapes=[pltpu.SemaphoreType.DMA((SPANS[index],))],
                compiler_params=pltpu.CompilerParams(vmem_limit_bytes=2 * MIB),
                cost_estimate=cost(2 * units * columns),
            )(in_hbm(down_codes), send)
            held.append(part)
            first += columns
        else:
            sign = signs[early.index(bit)]
        turned = turned * sign + other.astype(jnp.float32)
        send = turned.astype(jnp.bfloat16)

    order = [1] + [bit for bit in bits[1:]]
    spread = [0]
    for bit in reversed(order):
        spread = spread + [mask | bit for mask in spread]
    ahead = max(min((width - first) // SPAN, AHEAD), 1)
    keep, send = pl.pallas_call(
        functools.partial(down_kernel, 1.0 / math.sqrt(total_units), spread, len(held)),
        out_shape=(
            jax.ShapeDtypeStruct((devices // 2, own, tiles, LANES), jnp.float32),
            jax.ShapeDtypeStruct((devices // 2, own, tiles, LANES), jnp.bfloat16),
        ),
        in_specs=[VMEM, HBM] + [VMEM] * len(held),
        out_specs=(VMEM, VMEM),
        scratch_shapes=[
            pltpu.VMEM((count * tiles, LANES), jnp.float32),
            pltpu.VMEM((ahead, units, SPAN), jnp.bfloat16),
            pltpu.SemaphoreType.DMA((ahead,)),
        ],
        compiler_params=pltpu.CompilerParams(vmem_limit_bytes=20 * MIB),
        cost_estimate=cost(width * units, 2 * count * width * units),
    )(turned, in_hbm(down_codes), *[in_vmem(part) for part in held])
    summed = keep + swap(send, order[0]).astype(jnp.float32)
    for bit in order[1:]:
        half = summed.shape[0] // 2
        summed = summed[:half] + swap(summed[half:].astype(jnp.bfloat16), bit).astype(jnp.float32)
    return (summed.reshape(own, width) * down_scales[None, :]).astype(jnp.bfloat16)


def solution(mesh):
    in_specs = (
        P(("groups", "hx"), None),
        P(None, "hx"),
        P(None, "hx"),
        P(None, "hx"),
        P(None, "hx"),
        P("hx", None),
        P(),
        P(),
    )
    out_specs = P(("groups", "hx"), None)
    body = functools.partial(per_device, mesh.shape["groups"], mesh.shape["hx"])
    return jax.shard_map(body, mesh=mesh, in_specs=in_specs, out_specs=out_specs, check_vma=False)
```
